256 devices in a mesh: req: 64 (over z, x, core), tp: 4 (over y).
Axes of the slice: x: 4, y: 4, z: 8, core: 2. Of those that a mesh axis runs over, the one named last changes fastest.
Arguments:
- conv_input: bfloat16 [32768, 16384], P('req', 'tp'), may hold values from -6 to 6
- gate_input: bfloat16 [32768, 16384], P('req', 'tp'), may hold values from -6 to 6
- conv_weight: float32 [4, 16384], P(None, 'tp'), may hold values from -3 to 3
- conv_bias: float32 [16384], P('tp'), may hold values from -3 to 3
- select_weight: bfloat16 [16384, 288], P('tp'), may hold values from -0.046875 to 0.046875
- step_weight: bfloat16 [256, 16384], P(None, 'tp'), may hold values from -0.375 to 0.375
- step_bias: float32 [16384], P('tp'), may hold values from -7 to -2
- decay_log: float32 [16, 16384], P(None, 'tp'), may hold values from 0 to 2.8
- skip_gain: float32 [16384], P('tp'), may hold values from 0.5 to 1.5
- store_state: float32 [128, 64, 16, 256], P(None, 'req', None, 'tp'), may hold values from -4 to 4
- store_edge: bfloat16 [128, 64, 3, 256], P(None, 'req', None, 'tp'), may hold values from -6 to 6
- read_slot: int32 [64], replicated, may hold values from 0 to 127
- save_slot: int32 [64], replicated, may hold values from 0 to 127, as said below
- cache_hit: int32 [64], P('req'), may hold values 0 or 1
- suffix_length: int32 [64], P('req'), may hold values from 128 to 512, as said below
Outputs:
- gated: bfloat16 [32768, 16384], P('req', 'tp')
- new_state: float32 [128, 64, 16, 256], P(None, 'req', None, 'tp')
- new_edge_store: bfloat16 [128, 64, 3, 256], P(None, 'req', None, 'tp')
The draws below stay inside these ranges and needn't reach their ends.
Inputs may be any that keep to these rules, and one draw needn't show every extreme that they name: `save_slot`: the 64 entries are distinct. `suffix_length`: some request has exactly 512 live rows.
All inputs are finite; a program needn't handle non-finite values. No bound on the sum of `cache_hit` on one device may be relied on, other than what follows from the above.
Results may differ from the reference program's by a relative error of at most 0.007.
Values may be sent and summed in bfloat16 or wider, within the bound.
No kernel may reach another device: no remote copies, remote signals or barrier semaphores. Data moves between devices by JAX's collectives and lax.ppermute only.
A program may use at most 128 MiB of HBM per device.

```python
import jax
import jax.numpy as jnp
from jax import lax

INNER = 16384
STATE = 16
CONV = 4
RANK = 256
ROWS = 512
SLOTS = 128
STRIPE = 256
TOKENS = 32768
N_REQ = 64
N_TP = 4


def draw_save_slot(key, part):
    key = jax.random.fold_in(key, 11)
    key_middle, key_order = jax.random.split(key)
    middle = jax.random.permutation(key_middle, jnp.arange(1, SLOTS - 1, dtype=jnp.int32))
    chosen = jnp.concatenate([jnp.array([SLOTS - 1, 0], jnp.int32), middle[:N_REQ - 2]])
    return jax.random.permutation(key_order, chosen).astype(jnp.int32)


def draw_suffix_length(key, part):
    key = jax.random.fold_in(key, 12)
    key_lengths, key_longest = jax.random.split(key)
    lengths = jax.random.randint(key_lengths, (N_REQ,), ROWS // 4, ROWS + 1)
    longest = jax.random.randint(key_longest, (), 0, N_REQ)
    return lengths.at[longest].set(ROWS).astype(jnp.int32)


def plant(drawn, rng, smallest, largest):
    index_at = [jax.random.randint(jax.random.fold_in(rng, axis), (), 0, length) for axis, length in enumerate(drawn.shape)]
    widest = drawn.shape.index(max(drawn.shape))
    neighbour = index_at[:widest] + [(index_at[widest] + 1) % drawn.shape[widest]] + index_at[widest + 1:]
    return drawn.at[tuple(index_at)].set(smallest).at[tuple(neighbour)].set(largest)


def steps_of(key, dims, shards, low, top_value):
    def one(axis_at, parts):
        heights = jax.random.uniform(jax.random.fold_in(jax.random.fold_in(key, 6), axis_at), (parts,), jnp.float32, low / len(shards), top_value / len(shards))
        return jnp.repeat(jnp.exp(heights), dims[axis_at] // parts).reshape((-1,) + (1,) * (len(dims) - axis_at - 1))

    level = one(*shards[0])
    for cut in shards[1:]:
        level = level * one(*cut)
    return level


def noise(key, dims, spread, bound, cuts=(), held_as=jnp.bfloat16):
    loudness = steps_of(key, dims, cuts, -0.22, 0.18) if cuts else 1.0
    entries = jax.random.normal(key, dims, jnp.float32) * spread * loudness
    return jnp.minimum(jnp.maximum(entries, -bound), bound).astype(held_as)


def setup_inputs(seed: int = 0) -> dict:
    streams_of = jax.random.split(jax.random.key(seed), 16)
    return {
        "conv_input": noise(streams_of[0], (TOKENS, INNER), 1.0, 6.0, ((0, 64), (1, 4))),
        "gate_input": noise(streams_of[1], (TOKENS, INNER), 1.0, 6.0, ((0, 64), (1, 4))),
        "conv_weight": noise(streams_of[2], (CONV, INNER), CONV ** -0.5, 3.0, ((1, 4),), jnp.float32),
        "conv_bias": noise(streams_of[3], (INNER,), 0.5, 3.0, ((0, 4),), jnp.float32),
        "select_weight": noise(streams_of[4], (INNER, RANK + 2 * STATE), INNER ** -0.5, 0.046875, ((0, 4),)),
        "step_weight": noise(streams_of[5], (RANK, INNER), RANK ** -0.5, 0.375, ((1, 4),)),
        "step_bias": jnp.clip(-7.0 + 5.0 * jax.random.uniform(streams_of[6], (INNER,), jnp.float32) ** steps_of(streams_of[6], (INNER,), ((0, 4),), -0.2, 0.2), -7.0, -2.0),
        "decay_log": jnp.clip(2.8 * jax.random.uniform(streams_of[7], (STATE, INNER), jnp.float32) ** steps_of(streams_of[7], (STATE, INNER), ((1, 4),), -0.2, 0.2), 0.0, 2.8),
        "skip_gain": jnp.clip(0.5 + 1.0 * jax.random.uniform(streams_of[8], (INNER,), jnp.float32) ** steps_of(streams_of[8], (INNER,), ((0, 4),), -0.2, 0.2), 0.5, 1.5),
        "store_state": noise(streams_of[9], (SLOTS, N_REQ, STATE, STRIPE), 0.5, 4.0, ((1, 64), (3, 4)), jnp.float32),
        "store_edge": noise(streams_of[10], (SLOTS, N_REQ, CONV - 1, STRIPE), 1.0, 6.0, ((1, 64), (3, 4))),
        "read_slot": plant(jax.random.randint(streams_of[11], (N_REQ,), 0, SLOTS), jax.random.fold_in(streams_of[11], 1), 0, SLOTS - 1).astype(jnp.int32),
        "save_slot": draw_save_slot(jax.random.fold_in(streams_of[15], 71), 0),
        "cache_hit": plant((jax.random.randint(streams_of[13], (N_REQ,), 0, 4) < 3).astype(jnp.int32), jax.random.fold_in(streams_of[13], 1), 0, 1),
        "suffix_length": draw_suffix_length(jax.random.fold_in(streams_of[15], 71), 0),
    }


def to_tile(piece):
    count = piece.shape[1]
    return piece.reshape(N_REQ, count, N_TP, STRIPE // N_TP).transpose(1, 2, 0, 3).reshape(count, INNER)

def from_tile(tile):
    count = tile.shape[0]
    return tile.reshape(count, N_TP, N_REQ, STRIPE // N_TP).transpose(2, 0, 1, 3).reshape(N_REQ, count, STRIPE)

def reference(conv_input, gate_input, conv_weight, conv_bias, select_weight, step_weight, step_bias, decay_log, skip_gain, store_state, store_edge, read_slot, save_slot, cache_hit, suffix_length):
    decay_rate = -jnp.exp(decay_log)

    def one_request(pieces):
        rows_in, gates, slot, is_hit, length = pieces
        start_state = jnp.where(is_hit > 0, to_tile(store_state[slot]), jnp.zeros((STATE, INNER), jnp.float32))
        edge_rows = jnp.where(is_hit > 0, to_tile(store_edge[slot]), jnp.zeros((CONV - 1, INNER), jnp.bfloat16))
        padded = jnp.concatenate([edge_rows, rows_in], 0)
        conv_sum = conv_bias + jnp.zeros((ROWS, INNER), jnp.float32)
        for tap in range(CONV):
            conv_sum = conv_sum + conv_weight[tap] * padded[tap:tap + ROWS].astype(jnp.float32)
        mixed = jax.nn.silu(conv_sum)
        projected = jnp.dot(mixed.astype(jnp.bfloat16), select_weight, preferred_element_type=jnp.float32)
        low_part = projected[:, :RANK]
        normed = (low_part / jnp.sqrt(lax.optimization_barrier(jnp.mean(low_part * low_part, axis=-1, keepdims=True)) + 1e-06)).astype(jnp.bfloat16)
        live = (jnp.arange(ROWS) < length)[:, None]
        step_size = jax.nn.softplus(jnp.dot(normed, step_weight, preferred_element_type=jnp.float32) + step_bias)
        step_size = jnp.where(live, step_size, 0.0)
        drive = step_size * mixed

        def advance(state, row):
            size_row, drive_row, b_row, c_row = row
            state = jnp.exp(size_row[None, :] * decay_rate) * state + b_row[:, None] * drive_row[None, :]
            return (state, lax.optimization_barrier(jnp.sum(c_row[:, None] * state, axis=0)))
        end_state, scanned = lax.scan(advance, start_state, (step_size, drive, projected[:, RANK:RANK + STATE], projected[:, RANK + STATE:]))
        output = (scanned + skip_gain * mixed) * jax.nn.silu(gates.astype(jnp.float32))
        output = jnp.where(live, output, 0.0).astype(jnp.bfloat16)
        edge_next = lax.dynamic_slice_in_dim(padded, length.astype(jnp.int32), CONV - 1, 0)
        return (output, end_state, edge_next)
    outputs, end_states, edge_nexts = lax.map(one_request, (conv_input.reshape(N_REQ, ROWS, INNER), gate_input.reshape(N_REQ, ROWS, INNER), read_slot, cache_hit, suffix_length))
    new_state = store_state.at[save_slot].set(jax.vmap(from_tile)(end_states))
    new_edge_store = store_edge.at[save_slot].set(jax.vmap(from_tile)(edge_nexts))
    return (outputs.reshape(TOKENS, INNER), new_state, new_edge_store)
```

```python
import functools

import jax
import jax.numpy as jnp
from jax import lax
from jax.experimental import pallas as pl
from jax.experimental.pallas import tpu as pltpu
from jax.sharding import PartitionSpec as P

STATE = 16
CONV = 4
RANK = 256
HALO = 16
WIDE = 1024
LANES = 128
SUBLANES = 8
LOG2E = 1.4426950408889634
F32 = jnp.float32
BF16 = jnp.bfloat16
VMEM_LIMIT = 48 * 1024 * 1024


def conv_kernel(prev_ref, x_ref, weight_ref, bias_ref, select_ref, mixed_ref, part_ref, send_ref, rows_scr, low_scr):
    rows = x_ref.shape[0]
    groups = x_ref.shape[1] // LANES
    for group in range(groups):
        at = slice(group * LANES, (group + 1) * LANES)
        scr = rows_scr.at[group]
        scr[0:HALO, :] = prev_ref[:, at].astype(F32)
        scr[HALO : HALO + rows, :] = x_ref[:, at].astype(F32)
        total = bias_ref[:, at] + weight_ref[CONV - 1 : CONV, at] * scr[HALO : HALO + rows, :]
        for tap in range(CONV - 1):
            first = HALO - (CONV - 1) + tap
            total = total + weight_ref[tap : tap + 1, at] * scr[first : first + rows, :]
        mixed = total / (1.0 + jnp.exp(-total))
        mixed_ref[:, at] = mixed
        low_scr[:, at] = mixed.astype(BF16)
    part = lax.dot_general(
        select_ref[...], low_scr[...], (((1,), (1,)), ((), ())), preferred_element_type=F32
    ).T
    part_ref[...] = part
    send_ref[...] = part.astype(BF16)


def conv_rows(prev, x, weight, bias, select_t, first_row, n_rows, block):
    channels = x.shape[1]
    wide = select_t.shape[0]
    first = first_row // block
    if prev is None:
        prev = x
        prev_spec = pl.BlockSpec((HALO, channels), lambda i: ((first + i) * (block // HALO) - 1, 0))
    else:
        prev_spec = pl.BlockSpec((HALO, channels), lambda i: (0, 0))
    return pl.pallas_call(
        conv_kernel,
        grid=(n_rows // block,),
        in_specs=[
            prev_spec,
            pl.BlockSpec((block, channels), lambda i: (first + i, 0)),
            pl.BlockSpec((CONV, channels), lambda i: (0, 0)),
            pl.BlockSpec((1, channels), lambda i: (0, 0)),
            pl.BlockSpec((wide, channels), lambda i: (0, 0)),
        ],
        out_specs=[
            pl.BlockSpec((block, channels), lambda i: (i, 0)),
            pl.BlockSpec((block, wide), lambda i: (i, 0)),
            pl.BlockSpec((block, wide), lambda i: (i, 0)),
        ],
        out_shape=[
            jax.ShapeDtypeStruct((n_rows, channels), F32),
            jax.ShapeDtypeStruct((n_rows, wide), F32),
            jax.ShapeDtypeStruct((n_rows, wide), BF16),
        ],
        scratch_shapes=[
            pltpu.VMEM((channels // LANES, HALO + block, LANES), F32),
            pltpu.VMEM((block, channels), BF16),
        ],
        compiler_params=pltpu.CompilerParams(vmem_limit_bytes=VMEM_LIMIT),
        cost_estimate=pl.CostEstimate(
            flops=2 * n_rows * channels * wide,
            bytes_accessed=n_rows * channels * 24,
            transcendentals=2 * n_rows * channels,
        ),
        name="conv_rows",
    )(prev, x, weight, bias, select_t)


def scan_kernel(
    length_ref, own_ref, got1_ref, got2_ref, got3_ref, step_ref, bias_ref, decay_ref, skip_ref, mixed_ref, gate_ref,
    start_ref, *rest, first_row, aliased
):
    if aliased:
        rest = rest[1:]
    out_ref, end_ref, norm_scr, wide_scr, size_scr, drive_scr, scan_scr, state_scr, rate_scr = rest
    channel_block, row_block = pl.program_id(0), pl.program_id(1)
    rows = mixed_ref.shape[0]
    at_rows = pl.ds(pl.multiple_of(row_block * rows, rows), rows)

    @pl.when(channel_block == 0)
    def _():
        projected = (own_ref[...] + got1_ref[...].astype(F32)) + (
            got2_ref[...].astype(F32) + got3_ref[...].astype(F32)
        )
        low = projected[:, :RANK]
        scale = lax.rsqrt(jnp.mean(low * low, axis=-1, keepdims=True) + 1e-06)
        norm_scr[at_rows, :] = (low * scale).astype(BF16)
        picks = projected[:, RANK:]
        high = picks.astype(BF16)
        both = jnp.concatenate([high, (picks - high.astype(F32)).astype(BF16)], axis=1)
        shape = (4 * STATE, 2 * STATE * LANES)
        source = lax.broadcasted_iota(jnp.int32, shape, 0) % (2 * STATE)
        spread = (source == lax.broadcasted_iota(jnp.int32, shape, 1) // LANES).astype(BF16)
        wide_scr[at_rows, :] = jnp.dot(both, spread, preferred_element_type=F32)

    @pl.when(row_block == 0)
    def _():
        state_scr[...] = start_ref[0]
        rate = -jnp.exp(decay_ref[...]) * LOG2E
        for sub in range(SUBLANES):
            rate_scr[pl.ds(sub, STATE, stride=SUBLANES), :] = rate[:, sub * LANES : (sub + 1) * LANES]

    value = jnp.dot(norm_scr[at_rows, :], step_ref[...], preferred_element_type=F32) + bias_ref[...]
    row = first_row + row_block * rows + lax.broadcasted_iota(jnp.int32, (rows, 1), 0)
    live = row < length_ref[0]
    size = jnp.maximum(value, 0.0) + jnp.log1p(jnp.exp(-jnp.abs(value)))
    size = jnp.where(live, size, 0.0)
    drive = size * mixed_ref[...]
    for sub in range(SUBLANES):
        at = slice(sub * LANES, (sub + 1) * LANES)
        size_scr[pl.ds(sub, rows, stride=SUBLANES), :] = size[:, at]
        drive_scr[pl.ds(sub, rows, stride=SUBLANES), :] = drive[:, at]

    rates = [rate_scr[n * SUBLANES : (n + 1) * SUBLANES, :] for n in range(STATE)]

    def eight_rows(step, state):
        state = list(state)
        first = pl.multiple_of(row_block * rows + step * SUBLANES, SUBLANES)
        picks = wide_scr.at[pl.ds(first, SUBLANES), :]
        for position in range(SUBLANES):
            here = pl.ds(pl.multiple_of((step * SUBLANES + position) * SUBLANES, SUBLANES), SUBLANES)
            size_row, drive_row = size_scr[here, :], drive_scr[here, :]
            sums = [None, None]
            for n in range(STATE):
                b = jnp.broadcast_to(picks[position : position + 1, n * LANES : (n + 1) * LANES], (SUBLANES, LANES))
                m = STATE + n
                c = jnp.broadcast_to(picks[position : position + 1, m * LANES : (m + 1) * LANES], (SUBLANES, LANES))
                state[n] = jnp.exp2(size_row * rates[n]) * state[n] + b * drive_row
                term = c * state[n]
                sums[n % 2] = term if sums[n % 2] is None else sums[n % 2] + term
            scan_scr[here, :] = sums[0] + sums[1]
        return tuple(state)

    state = lax.fori_loop(0, rows // SUBLANES, eight_rows, tuple(state_scr[n] for n in range(STATE)))
    for n in range(STATE):
        state_scr[n] = state[n]

    gate = gate_ref[...].astype(F32)
    gate = gate / (1.0 + jnp.exp(-gate))
    direct = skip_ref[...] * mixed_ref[...]
    for sub in range(SUBLANES):
        at = slice(sub * LANES, (sub + 1) * LANES)
        scanned = scan_scr[pl.ds(sub, rows, stride=SUBLANES), :]
        out_ref[:, at] = jnp.where(live, (scanned + direct[:, at]) * gate[:, at], 0.0).astype(BF16)

    @pl.when(row_block == pl.num_programs(1) - 1)
    def _():
        end_ref[0] = state_scr[...]


def scan_rows(length, parts, step_weight, step_bias, decay_log, skip_gain, mixed, gate, start, out, first_row, block):
    n_rows, channels = mixed.shape
    blocks = channels // WIDE
    first = first_row // block
    wide = parts[0].shape[1]
    by_channel = lambda c, i, *_: (0, c)
    part_spec = pl.BlockSpec((block, wide), lambda c, i, *_: (jnp.where(c == 0, i, 0), 0))
    state_spec = pl.BlockSpec((1, STATE, SUBLANES, LANES), lambda c, i, *_: (c, 0, 0, 0))
    operands = [length, *parts, step_weight, step_bias, decay_log, skip_gain, mixed, gate, start]
    in_specs = [part_spec] * 4 + [
        pl.BlockSpec((RANK, WIDE), by_channel),
        pl.BlockSpec((1, WIDE), by_channel),
        pl.BlockSpec((STATE, WIDE), by_channel),
        pl.BlockSpec((1, WIDE), by_channel),
        pl.BlockSpec((block, WIDE), lambda c, i, *_: (i, c)),
        pl.BlockSpec((block, WIDE), lambda c, i, *_: (first + i, c)),
        state_spec,
    ]
    aliases = {}
    if out is not None:
        aliases = {len(operands): 0}
        operands.append(out)
        in_specs.append(pl.BlockSpec(memory_space=pl.ANY))
    return pl.pallas_call(
        functools.partial(scan_kernel, first_row=first_row, aliased=out is not None),
        grid_spec=pltpu.PrefetchScalarGridSpec(
            num_scalar_prefetch=1,
            grid=(blocks, n_rows // block),
            in_specs=in_specs,
            out_specs=[pl.BlockSpec((block, WIDE), lambda c, i, *_: (first + i, c)), state_spec],
            scratch_shapes=[
                pltpu.VMEM((n_rows, RANK), BF16),
                pltpu.VMEM((n_rows, 2 * STATE * LANES), F32),
                pltpu.VMEM((block * SUBLANES, LANES), F32),
                pltpu.VMEM((block * SUBLANES, LANES), F32),
                pltpu.VMEM((block * SUBLANES, LANES), F32),
                pltpu.VMEM((STATE, SUBLANES, LANES), F32),
                pltpu.VMEM((STATE * SUBLANES, LANES), F32),
            ],
        ),
        out_shape=[
            jax.ShapeDtypeStruct(gate.shape, BF16),
            jax.ShapeDtypeStruct((blocks, STATE, SUBLANES, LANES), F32),
        ],
        input_output_aliases=aliases,
        compiler_params=pltpu.CompilerParams(vmem_limit_bytes=VMEM_LIMIT),
        cost_estimate=pl.CostEstimate(
            flops=2 * n_rows * channels * RANK + 100 * n_rows * channels * STATE,
            bytes_accessed=n_rows * channels * 8,
            transcendentals=n_rows * channels * STATE,
        ),
        name="scan_rows",
    )(*operands)


def from_others(sent, n_tp):
    return [lax.ppermute(sent, "tp", [(d, (d + s) % n_tp) for d in range(n_tp)]) for s in range(1, n_tp)]


def local(
    n_req,
    n_tp,
    conv_input,
    gate_input,
    conv_weight,
    conv_bias,
    select_weight,
    step_weight,
    step_bias,
    decay_log,
    skip_gain,
    store_state,
    store_edge,
    read_slot,
    save_slot,
    cache_hit,
    suffix_length,
):
    local_rows, channels = conv_input.shape
    slots, _, _, stripe = store_state.shape
    edge_rows = CONV - 1
    n_state, n_edge = STATE * stripe, edge_rows * stripe
    is_hit = cache_hit[0] > 0
    length = suffix_length[0]
    store = store_state.transpose(1, 2, 3, 0).reshape(n_state, slots)
    edges = store_edge.transpose(1, 2, 3, 0).reshape(n_edge, slots)

    slot_ids = jnp.arange(slots, dtype=jnp.int32)
    reads = (read_slot[:, None] == slot_ids[None, :]).astype(BF16)
    contract_slots = (((1,), (1,)), ((), ()))
    held_state = lax.dot_general(reads, store.astype(BF16), contract_slots, preferred_element_type=F32)
    held_edge = lax.dot_general(reads, edges, contract_slots, preferred_element_type=F32)
    edge_next = lax.dynamic_slice_in_dim(conv_input, length - edge_rows, edge_rows, 0)
    edge_next = edge_next.reshape(edge_rows, n_req, stripe).transpose(1, 0, 2).reshape(n_req, n_edge)
    outgoing = jnp.concatenate([held_state.astype(BF16), held_edge.astype(BF16), edge_next], axis=1)
    arrived = lax.all_to_all(outgoing, "req", split_axis=0, concat_axis=0, tiled=True)

    select_t = select_weight.T
    conv_bias = conv_bias.reshape(1, channels)
    step_bias = step_bias.reshape(1, channels)
    skip_gain = skip_gain.reshape(1, channels)
    block = min(128, local_rows // 2)
    conv = functools.partial(conv_rows, block=block)
    late_mixed, late_part, late_send = conv(
        None, conv_input, conv_weight, conv_bias, select_t, block, local_rows - block
    )
    late_parts = [late_part] + from_others(late_send, n_tp)

    got = jnp.where(is_hit, arrived[:, : n_state + n_edge], 0)
    start = got[:, :n_state].astype(F32).reshape(n_req, STATE, stripe).transpose(1, 0, 2)
    start = start.reshape(STATE, channels // WIDE, SUBLANES, LANES).transpose(1, 0, 2, 3)
    edge = got[:, n_state:].reshape(n_req, edge_rows, stripe).transpose(1, 0, 2).reshape(edge_rows, channels)
    edge = jnp.pad(edge, ((HALO - edge_rows, 0), (0, 0)))
    early_mixed, early_part, early_send = conv(edge, conv_input, conv_weight, conv_bias, select_t, 0, block)
    early_parts = [early_part] + from_others(early_send, n_tp)

    scan = functools.partial(scan_rows, block=block)
    shared = (step_weight, step_bias, decay_log, skip_gain)
    out, state = scan(suffix_length, early_parts, *shared, early_mixed, gate_input, start, None, 0)
    out, state = scan(suffix_length, late_parts, *shared, late_mixed, gate_input, state, out, block)

    back = state.astype(BF16).reshape(channels // WIDE, STATE, SUBLANES, LANES // stripe, stripe)
    back = back.transpose(0, 2, 3, 1, 4).reshape(n_req, n_state)
    back = lax.all_to_all(back, "req", split_axis=0, concat_axis=0, tiled=True)
    saves = (save_slot[:, None] == slot_ids[None, :]).astype(BF16)
    saved = jnp.any(save_slot[:, None] == slot_ids[None, :], axis=0)[None, :]
    contract_requests = (((0,), (0,)), ((), ()))
    new_store = lax.dot_general(back, saves, contract_requests, preferred_element_type=F32)
    new_store = jnp.where(saved, new_store, store)
    new_edges = lax.dot_general(
        arrived[:, n_state + n_edge :], saves, contract_requests, preferred_element_type=F32
    ).astype(BF16)
    new_edges = jnp.where(saved, new_edges, edges)
    new_state = new_store.reshape(1, STATE, stripe, slots).transpose(3, 0, 1, 2)
    new_edge_store = new_edges.reshape(1, edge_rows, stripe, slots).transpose(3, 0, 1, 2)
    return (out, new_state, new_edge_store)


def solution(mesh):
    placed = (
        P("req", "tp"),
        P("req", "tp"),
        P(None, "tp"),
        P("tp"),
        P("tp", None),
        P(None, "tp"),
        P("tp"),
        P(None, "tp"),
        P("tp"),
        P(None, "req", None, "tp"),
        P(None, "req", None, "tp"),
        P(),
        P(),
        P("req"),
        P("req"),
    )
    return jax.shard_map(
        functools.partial(local, mesh.shape["req"], mesh.shape["tp"]),
        mesh=mesh,
        in_specs=placed,
        out_specs=(P("req", "tp"), P(None, "req", None, "tp"), P(None, "req", None, "tp")),
        check_vma=False,
    )
```

```python
import functools

import jax
import jax.numpy as jnp
from jax import lax
from jax.experimental import pallas as pl
from jax.experimental.pallas import tpu as pltpu
from jax.sharding import PartitionSpec as P

STATE = 16
CONV = 4
RANK = 256
HALO = 16
WIDE = 1024
LANES = 128
SUBLANES = 8
LOG2E = 1.4426950408889634
F32 = jnp.float32
BF16 = jnp.bfloat16
HALF = 64
EDGE_AT = 8
NEXT_AT = 11
CHUNK = 16
FETCHES = 6
GROUPS_AT_ONCE = 4
VMEM_LIMIT = 60 * 1024 * 1024
SMALL_LIMIT = 24 * 1024 * 1024


def low_half():
    return lax.broadcasted_iota(jnp.int32, (1, LANES), 1) < HALF


def silu(v):
    half = 0.5 * v
    return half + half * jnp.tanh(half)


def pack_kernel(length_ref, read_ref, store_ref, edge_ref, x_ref, out_ref, tiles_scr, low_scr, rows_scr, sem):
    n_req = read_ref.shape[1]
    slots = store_ref.shape[1]
    edge_rows = CONV - 1
    last = length_ref[0] - edge_rows
    first = pl.multiple_of(jnp.minimum(last // HALO * HALO, x_ref.shape[0] - 2 * HALO), HALO)
    copy = pltpu.make_async_copy(x_ref.at[pl.ds(first, 2 * HALO), :], low_scr, sem)
    copy.start()
    reads = (lax.broadcasted_iota(jnp.int32, (slots, n_req), 0) == read_ref[...]).astype(BF16)
    for row in range(STATE // 2):
        held = lax.dot_general(
            reads, store_ref[row * LANES : (row + 1) * LANES, :].astype(BF16), (((0,), (1,)), ((), ())),
            preferred_element_type=F32,
        )
        tiles_scr[pl.ds(row, n_req, stride=CHUNK), :] = held
    for row in range(edge_rows):
        edge = edge_ref[row * HALF : (row + 1) * HALF, :]
        held = lax.dot_general(
            reads, jnp.concatenate([edge, edge], axis=0), (((0,), (1,)), ((), ())), preferred_element_type=F32
        )
        tiles_scr[pl.ds(EDGE_AT + row, n_req, stride=CHUNK), :] = held
    for row in range(NEXT_AT + edge_rows, CHUNK):
        tiles_scr[pl.ds(row, n_req, stride=CHUNK), :] = jnp.zeros((n_req, LANES), F32)
    copy.wait()
    rows_scr[...] = low_scr[...].astype(F32)
    for row in range(edge_rows):
        line = rows_scr[pl.ds(last - first + row, 1), :]
        for req in range(n_req):
            at = req // 2 * LANES
            tiles_scr[req * CHUNK + NEXT_AT + row : req * CHUNK + NEXT_AT + row + 1, :] = line[:, at : at + LANES]
    out_ref[...] = tiles_scr[...].astype(BF16).reshape(out_ref.shape)


def pack(length, read_slot, store, edges, x):
    n_req = read_slot.shape[0]
    channels = x.shape[1]
    whole = lambda *_: (0, 0)
    return pl.pallas_call(
        pack_kernel,
        grid_spec=pltpu.PrefetchScalarGridSpec(
            num_scalar_prefetch=1,
            grid=(1,),
            in_specs=[
                pl.BlockSpec((1, n_req), whole),
                pl.BlockSpec(store.shape, whole),
                pl.BlockSpec(edges.shape, whole),
                pl.BlockSpec(memory_space=pl.ANY),
            ],
            out_specs=pl.BlockSpec((n_req, CHUNK, LANES), lambda *_: (0, 0, 0)),
            scratch_shapes=[
                pltpu.VMEM((n_req * CHUNK, LANES), F32),
                pltpu.VMEM((2 * HALO, channels), BF16),
                pltpu.VMEM((2 * HALO, channels), F32),
                pltpu.SemaphoreType.DMA,
            ],
        ),
        out_shape=jax.ShapeDtypeStruct((n_req, CHUNK, LANES), BF16),
        compiler_params=pltpu.CompilerParams(vmem_limit_bytes=VMEM_LIMIT),
        name="pack",
    )(length, read_slot.reshape(1, n_req), store, edges, x)


def conv_block(prev, x_ref, weight_ref, bias_ref, select_hbm, mixed_ref, part_ref, send_ref, rows_scr, select_ref, sems):
    rows = x_ref.shape[0]
    groups = x_ref.shape[1] // LANES
    is_first = pl.program_id(0) == 0
    height = select_ref.shape[0] // FETCHES
    copies = [
        pltpu.make_async_copy(
            select_hbm.at[k * height : (k + 1) * height, :], select_ref.at[k * height : (k + 1) * height, :], sems.at[k]
        )
        for k in range(FETCHES)
    ]

    @pl.when(is_first)
    def _():
        for copy in copies:
            copy.start()

    def some_groups(step, _):
        for k in range(GROUPS_AT_ONCE):
            group = step * GROUPS_AT_ONCE + k
            at = pl.ds(pl.multiple_of(group * LANES, LANES), LANES)
            scr = rows_scr.at[k]
            scr[0:HALO, :] = prev(group)
            scr[HALO : HALO + rows, :] = x_ref[:, at].astype(F32)
            total = bias_ref[:, at] + weight_ref[CONV - 1 : CONV, at] * scr[HALO : HALO + rows, :]
            for tap in range(CONV - 1):
                first = HALO - (CONV - 1) + tap
                total = total + weight_ref[tap : tap + 1, at] * scr[first : first + rows, :]
            mixed_ref[:, at] = silu(total).astype(BF16)
        return 0

    lax.fori_loop(0, groups // GROUPS_AT_ONCE, some_groups, 0)

    @pl.when(is_first)
    def _():
        for copy in copies:
            copy.wait()

    part = lax.dot_general(
        select_ref[...], mixed_ref[...], (((1,), (1,)), ((), ())), preferred_element_type=F32
    ).T
    part_ref[...] = part
    send_ref[...] = part.astype(BF16)


def late_kernel(prev_ref, x_ref, weight_ref, bias_ref, select_ref, mixed_ref, part_ref, send_ref, *scr):
    prev = lambda group: prev_ref[:, pl.ds(pl.multiple_of(group * LANES, LANES), LANES)].astype(F32)
    conv_block(prev, x_ref, weight_ref, bias_ref, select_ref, mixed_ref, part_ref, send_ref, *scr)


def early_kernel(
    hit_ref, arrived_ref, after_ref, x_ref, weight_ref, bias_ref, select_ref, mixed_ref, part_ref, send_ref, start_ref,
    tiles_scr, edge_scr, *scr
):
    del after_ref
    hit = hit_ref[0] > 0
    n_req = arrived_ref.shape[0]
    pairs = n_req // 2
    tiles = arrived_ref[...].astype(F32).reshape(n_req * CHUNK, LANES)
    tiles_scr[...] = jnp.where(hit, tiles, 0.0)
    low = low_half()
    even = lambda row: tiles_scr[pl.ds(row, pairs, stride=2 * CHUNK), :]
    odd = lambda row: tiles_scr[pl.ds(CHUNK + row, pairs, stride=2 * CHUNK), :]
    for row in range(STATE // 2):
        a, b = even(row), odd(row)
        first, second = jnp.where(low, a, pltpu.roll(b, HALF, 1)), jnp.where(low, pltpu.roll(a, HALF, 1), b)
        for block in range(pairs // SUBLANES):
            at = slice(block * SUBLANES, (block + 1) * SUBLANES)
            start_ref[block, 2 * row] = first[at]
            start_ref[block, 2 * row + 1] = second[at]
    edge_scr[...] = jnp.zeros(edge_scr.shape, F32)
    for row in range(CONV - 1):
        edge_scr[pl.ds(HALO - (CONV - 1) + row, pairs, stride=HALO), :] = jnp.where(low, even(EDGE_AT + row), odd(EDGE_AT + row))
    prev = lambda group: edge_scr[pl.ds(pl.multiple_of(group * HALO, HALO), HALO), :]
    conv_block(prev, x_ref, weight_ref, bias_ref, select_ref, mixed_ref, part_ref, send_ref, *scr)


def conv_rows(x, weight, bias, select_t, first_row, n_rows, block, arrived=None, hit=None, after=None):
    channels = x.shape[1]
    wide = select_t.shape[0]
    first = first_row // block
    fixed = lambda *_: (0, 0)
    in_specs = [
        pl.BlockSpec((block, channels), lambda i, *_: (first + i, 0)),
        pl.BlockSpec((CONV, channels), fixed),
        pl.BlockSpec((1, channels), fixed),
        pl.BlockSpec(memory_space=pl.ANY),
    ]
    out_specs = [
        pl.BlockSpec((block, channels), lambda i, *_: (i, 0)),
        pl.BlockSpec((block, wide), lambda i, *_: (i, 0)),
        pl.BlockSpec((block, wide), lambda i, *_: (i, 0)),
    ]
    out_shape = [
        jax.ShapeDtypeStruct((n_rows, channels), BF16),
        jax.ShapeDtypeStruct((n_rows, wide), F32),
        jax.ShapeDtypeStruct((n_rows, wide), BF16),
    ]
    scratch = [
        pltpu.VMEM((GROUPS_AT_ONCE, HALO + block, LANES), F32),
        pltpu.VMEM(select_t.shape, BF16),
        pltpu.SemaphoreType.DMA((FETCHES,)),
    ]
    operands = [x, weight, bias, select_t]
    if arrived is None:
        kernel, name, scalars = late_kernel, "conv_late", []
        in_specs = [
            pl.BlockSpec((HALO, channels), lambda i, *_: ((first + i) * (block // HALO) - 1, 0))
        ] + in_specs
        operands = [x] + operands
    else:
        kernel, name, scalars = early_kernel, "conv_early", [hit]
        n_req = arrived.shape[0]
        in_specs = [
            pl.BlockSpec(arrived.shape, lambda *_: (0, 0, 0)),
            pl.BlockSpec(memory_space=pl.ANY),
        ] + in_specs
        operands = [arrived, after] + operands
        start_shape = (channels // WIDE, STATE, SUBLANES, LANES)
        out_specs.append(pl.BlockSpec(start_shape, lambda *_: (0, 0, 0, 0)))
        out_shape.append(jax.ShapeDtypeStruct(start_shape, F32))
        scratch = [
            pltpu.VMEM((n_req * CHUNK, LANES), F32),
            pltpu.VMEM((channels // LANES * HALO, LANES), F32),
        ] + scratch
    return pl.pallas_call(
        kernel,
        grid_spec=pltpu.PrefetchScalarGridSpec(
            num_scalar_prefetch=len(scalars),
            grid=(n_rows // block,),
            in_specs=in_specs,
            out_specs=out_specs,
            scratch_shapes=scratch,
        ),
        out_shape=out_shape,
        compiler_params=pltpu.CompilerParams(vmem_limit_bytes=VMEM_LIMIT),
        cost_estimate=pl.CostEstimate(
            flops=2 * n_rows * channels * wide,
            bytes_accessed=n_rows * channels * 24,
            transcendentals=2 * n_rows * channels,
        ),
        name=name,
    )(*scalars, *operands)


def scan_kernel(
    length_ref, *refs, n_parts, first_row, aliased, packed
):
    part_refs, refs = refs[:n_parts], refs[n_parts:]
    step_ref, bias_ref, decay_ref, skip_ref, mixed_ref, gate_ref, start_ref, *refs = refs
    if aliased:
        refs = refs[1:]
    out_ref, end_ref, norm_scr, wide_scr, value_scr, state_scr, rate_scr, back_scr, *lines = refs
    sizes, drives, scans = lines[0:2], lines[2:4], lines[4:6]
    channel_block, row_block = pl.program_id(0), pl.program_id(1)
    rows = mixed_ref.shape[0]
    pairs = rows // HALO
    at_rows = pl.ds(pl.multiple_of(row_block * rows, rows), rows)

    @pl.when(channel_block == 0)
    def _():
        projected = part_refs[0][...].astype(F32)
        for part_ref in part_refs[1:]:
            projected = projected + part_ref[...].astype(F32)
        low = projected[:, :RANK]
        scale = lax.rsqrt(jnp.mean(low * low, axis=-1, keepdims=True) + 1e-06)
        norm_scr[at_rows, :] = (low * scale).astype(BF16)
        picks = projected[:, RANK:]
        high = picks.astype(BF16)
        both = jnp.concatenate([high, (picks - high.astype(F32)).astype(BF16)], axis=1)
        shape = (4 * STATE, 2 * STATE * LANES)
        source = lax.broadcasted_iota(jnp.int32, shape, 0) % (2 * STATE)
        spread = (source == lax.broadcasted_iota(jnp.int32, shape, 1) // LANES).astype(BF16)
        wide_scr[at_rows, :] = jnp.dot(both, spread, preferred_element_type=F32)

    @pl.when(row_block == 0)
    def _():
        state_scr[...] = start_ref[0]
        rate = -jnp.exp(decay_ref[...]) * LOG2E
        for sub in range(SUBLANES):
            rate_scr[pl.ds(sub, STATE, stride=SUBLANES), :] = rate[:, sub * LANES : (sub + 1) * LANES]

    value_scr[...] = jnp.dot(norm_scr[at_rows, :], step_ref[...], preferred_element_type=F32)
    rates = [rate_scr[n * SUBLANES : (n + 1) * SUBLANES, :] for n in range(STATE)]
    row_in_tile = lax.broadcasted_iota(jnp.int32, (SUBLANES, LANES), 0)
    left = length_ref[0] - first_row - row_block * rows

    def steps_of(pair, tile):
        first = pl.multiple_of(pair * HALO, HALO)
        live = row_in_tile < left - first - tile * SUBLANES
        for sub in range(SUBLANES):
            at = slice(sub * LANES, (sub + 1) * LANES)
            value = value_scr[pl.ds(first + tile * SUBLANES, SUBLANES), at] + bias_ref[:, at]
            small = jnp.exp2(jnp.abs(value) * -LOG2E)
            soft = jnp.where(small < 4e-3, small - 0.5 * small * small, jnp.log(1.0 + small))
            size = jnp.where(live, jnp.maximum(value, 0.0) + soft, 0.0)
            mixed = mixed_ref[pl.ds(first, HALO), at].astype(F32)[tile * SUBLANES : (tile + 1) * SUBLANES]
            sizes[tile][pl.ds(sub, SUBLANES, stride=SUBLANES), :] = size
            drives[tile][pl.ds(sub, SUBLANES, stride=SUBLANES), :] = size * mixed

    def advance(state, pair, tile):
        state = list(state)
        first = pl.multiple_of(row_block * rows + pair * HALO + tile * SUBLANES, SUBLANES)
        picks = wide_scr.at[pl.ds(first, SUBLANES), :]
        for position in range(SUBLANES):
            here = slice(position * SUBLANES, (position + 1) * SUBLANES)
            size_row, drive_row = sizes[tile][here, :], drives[tile][here, :]
            sums = [None, None]
            for n in range(STATE):
                b = jnp.broadcast_to(picks[position : position + 1, n * LANES : (n + 1) * LANES], (SUBLANES, LANES))
                m = STATE + n
                c = jnp.broadcast_to(picks[position : position + 1, m * LANES : (m + 1) * LANES], (SUBLANES, LANES))
                state[n] = jnp.exp2(size_row * rates[n]) * state[n] + b * drive_row
                term = c * state[n]
                sums[n % 2] = term if sums[n % 2] is None else sums[n % 2] + term
            scans[tile][here, :] = sums[0] + sums[1]
        return tuple(state)

    def gate_of(pair):
        first = pl.multiple_of(pair * HALO, HALO)
        here = pl.ds(first, HALO)
        for sub in range(SUBLANES):
            at = slice(sub * LANES, (sub + 1) * LANES)
            scanned = jnp.concatenate(
                [scans[tile][pl.ds(sub, SUBLANES, stride=SUBLANES), :] for tile in range(2)], axis=0
            )
            value = scanned + skip_ref[:, at] * mixed_ref[here, at].astype(F32)
            value = value * silu(gate_ref[here, at].astype(F32))
            live = jnp.concatenate([row_in_tile, row_in_tile + SUBLANES], axis=0) < left - first
            out_ref[here, at] = jnp.where(live, value, 0.0).astype(BF16)

    def one_pair(pair, state):
        gate_of(jnp.maximum(pair - 1, 0))
        steps_of(pair, 1)
        state = advance(state, pair, 0)
        steps_of(jnp.minimum(pair + 1, pairs - 1), 0)
        return advance(state, pair, 1)

    steps_of(0, 0)
    state = lax.fori_loop(0, pairs, one_pair, tuple(state_scr[n] for n in range(STATE)))
    gate_of(pairs - 1)
    for n in range(STATE):
        state_scr[n] = state[n]

    @pl.when(row_block == pl.num_programs(1) - 1)
    def _():
        if packed:
            low = low_half()
            for row in range(STATE // 2):
                a, b = state_scr[2 * row], state_scr[2 * row + 1]
                even = jnp.where(low, a, pltpu.roll(b, HALF, 1))
                odd = jnp.where(low, pltpu.roll(a, HALF, 1), b)
                back_scr[pl.ds(row, SUBLANES, stride=2 * SUBLANES), :] = even
                back_scr[pl.ds(SUBLANES + row, SUBLANES, stride=2 * SUBLANES), :] = odd
            end_ref[...] = back_scr[...].astype(BF16).reshape(end_ref.shape)
        else:
            end_ref[0] = state_scr[...]


def scan_rows(length, parts, step_weight, step_bias, decay_log, skip_gain, mixed, gate, start, out, first_row, block):
    n_rows, channels = mixed.shape
    blocks = channels // WIDE
    first = first_row // block
    wide = parts[0].shape[1]
    packed = first_row > 0
    by_channel = lambda c, i, *_: (0, c)
    part_spec = pl.BlockSpec((block, wide), lambda c, i, *_: (jnp.where(c == 0, i, 0), 0))
    state_shape = (1, STATE, SUBLANES, LANES)
    state_spec = pl.BlockSpec(state_shape, lambda c, i, *_: (c, 0, 0, 0))
    operands = [length, *parts, step_weight, step_bias, decay_log, skip_gain, mixed, gate, start]
    in_specs = [part_spec] * len(parts) + [
        pl.BlockSpec((RANK, WIDE), by_channel),
        pl.BlockSpec((1, WIDE), by_channel),
        pl.BlockSpec((STATE, WIDE), by_channel),
        pl.BlockSpec((1, WIDE), by_channel),
        pl.BlockSpec((block, WIDE), lambda c, i, *_: (i, c)),
        pl.BlockSpec((block, WIDE), lambda c, i, *_: (first + i, c)),
        state_spec,
    ]
    aliases = {}
    if out is not None:
        aliases = {len(operands): 0}
        operands.append(out)
        in_specs.append(pl.BlockSpec(memory_space=pl.ANY))
    if packed:
        per_block = WIDE // HALF
        end_spec = pl.BlockSpec((per_block, SUBLANES, LANES), lambda c, i, *_: (c, 0, 0))
        end_shape = jax.ShapeDtypeStruct((blocks * per_block, SUBLANES, LANES), BF16)
    else:
        end_spec = state_spec
        end_shape = jax.ShapeDtypeStruct((blocks, *state_shape[1:]), F32)
    return pl.pallas_call(
        functools.partial(
            scan_kernel, n_parts=len(parts), first_row=first_row, aliased=out is not None, packed=packed
        ),
        grid_spec=pltpu.PrefetchScalarGridSpec(
            num_scalar_prefetch=1,
            grid=(blocks, n_rows // block),
            in_specs=in_specs,
            out_specs=[pl.BlockSpec((block, WIDE), lambda c, i, *_: (first + i, c)), end_spec],
            scratch_shapes=[
                pltpu.VMEM((n_rows, RANK), BF16),
                pltpu.VMEM((n_rows, 2 * STATE * LANES), F32),
                pltpu.VMEM((block, WIDE), F32),
                pltpu.VMEM((STATE, SUBLANES, LANES), F32),
                pltpu.VMEM((STATE * SUBLANES, LANES), F32),
                pltpu.VMEM((WIDE // HALF * SUBLANES, LANES), F32),
            ]
            + [pltpu.VMEM((SUBLANES * SUBLANES, LANES), F32)] * 6,
        ),
        out_shape=[jax.ShapeDtypeStruct(gate.shape, BF16), end_shape],
        input_output_aliases=aliases,
        compiler_params=pltpu.CompilerParams(vmem_limit_bytes=VMEM_LIMIT),
        cost_estimate=pl.CostEstimate(
            flops=2 * n_rows * channels * RANK + 100 * n_rows * channels * STATE,
            bytes_accessed=n_rows * channels * 8,
            transcendentals=n_rows * channels * STATE,
        ),
        name="scan_rows",
    )(*operands)


def save_kernel(slot_ref, half_ref, tiles_ref, store_ref, out_ref, tiles_scr, *, n_rows, first_row, halves):
    n_req, chunk, _ = tiles_ref.shape
    slots = store_ref.shape[1]
    saves = slot_ref[...] == lax.broadcasted_iota(jnp.int32, (n_req, slots), 1)
    saved = jnp.max(saves.astype(F32), axis=0, keepdims=True) > 0.0
    saves = saves.astype(BF16)
    tiles = tiles_ref[...].astype(F32).reshape(n_req * chunk, LANES)
    if halves:
        tiles = jnp.where(half_ref[0] > 0, pltpu.roll(tiles, HALF, 1), tiles)
    tiles_scr[...] = tiles
    height = HALF if halves else LANES
    for row in range(n_rows):
        new = tiles_scr[pl.ds(first_row + row, n_req, stride=chunk), :].astype(BF16)
        new = lax.dot_general(new, saves, (((0,), (0,)), ((), ())), preferred_element_type=F32)[:height]
        at = slice(row * height, (row + 1) * height)
        out_ref[at, :] = jnp.where(saved, new, store_ref[at, :].astype(F32)).astype(out_ref.dtype)


def save(save_slot, half, tiles, store, n_rows, first_row, halves):
    n_req, chunk, _ = tiles.shape
    whole = lambda *_: (0, 0)
    return pl.pallas_call(
        functools.partial(save_kernel, n_rows=n_rows, first_row=first_row, halves=halves),
        grid=(1,),
        in_specs=[
            pl.BlockSpec((n_req, 1), whole),
            pl.BlockSpec(memory_space=pltpu.SMEM),
            pl.BlockSpec(tiles.shape, lambda *_: (0, 0, 0)),
            pl.BlockSpec(store.shape, whole),
        ],
        out_specs=pl.BlockSpec(store.shape, whole),
        out_shape=jax.ShapeDtypeStruct(store.shape, store.dtype),
        scratch_shapes=[pltpu.VMEM((n_req * chunk, LANES), F32)],
        compiler_params=pltpu.CompilerParams(vmem_limit_bytes=SMALL_LIMIT),
        name="save",
    )(save_slot.reshape(n_req, 1), half, tiles, store)


def from_others(part, sent, n_tp):
    return [part] + [
        lax.ppermute(sent, "tp", [(d, (d + s) % n_tp) for d in range(n_tp)]) for s in range(1, n_tp)
    ]


def local(
    n_tp,
    conv_input,
    gate_input,
    conv_weight,
    conv_bias,
    select_weight,
    step_weight,
    step_bias,
    decay_log,
    skip_gain,
    store_state,
    store_edge,
    read_slot,
    save_slot,
    cache_hit,
    suffix_length,
):
    local_rows, channels = conv_input.shape
    slots, _, _, stripe = store_state.shape
    edge_rows = CONV - 1
    store = store_state.transpose(1, 2, 3, 0).reshape(STATE * stripe, slots)
    edges = store_edge.transpose(1, 2, 3, 0).reshape(edge_rows * stripe, slots)
    outgoing = pack(suffix_length, read_slot, store, edges, conv_input)
    arrived = lax.all_to_all(outgoing, "req", split_axis=0, concat_axis=0, tiled=True)

    select_t = select_weight.T
    conv_bias = conv_bias.reshape(1, channels)
    step_bias = step_bias.reshape(1, channels)
    skip_gain = skip_gain.reshape(1, channels)
    block = 128
    late_mixed, late_part, late_sent = conv_rows(
        conv_input, conv_weight, conv_bias, select_t, block, local_rows - block, block
    )
    late_parts = from_others(late_part, late_sent, n_tp)
    early_mixed, early_part, early_sent, start = conv_rows(
        conv_input, conv_weight, conv_bias, select_t, 0, block, block, arrived, cache_hit, late_part
    )
    early_parts = from_others(early_part, early_sent, n_tp)

    scan = functools.partial(scan_rows, block=block)
    shared = (step_weight, step_bias, decay_log, skip_gain)
    out, state = scan(suffix_length, early_parts, *shared, early_mixed, gate_input, start, None, 0)
    out, back = scan(suffix_length, late_parts, *shared, late_mixed, gate_input, state, out, block)

    half = (lax.axis_index("req") % 2).astype(jnp.int32).reshape(1)
    arrived, back = lax.optimization_barrier((arrived, back))
    new_edges = save(save_slot, half, arrived, edges, edge_rows, NEXT_AT, True)
    new_edges, back = lax.optimization_barrier((new_edges, back))
    back = lax.all_to_all(back, "req", split_axis=0, concat_axis=0, tiled=True)
    new_store = save(save_slot, half, back, store, STATE // 2, 0, False)
    new_state = new_store.reshape(1, STATE, stripe, slots).transpose(3, 0, 1, 2)
    new_edge_store = new_edges.reshape(1, edge_rows, stripe, slots).transpose(3, 0, 1, 2)
    return (out, new_state, new_edge_store)


def solution(mesh):
    placed = (
        P("req", "tp"),
        P("req", "tp"),
        P(None, "tp"),
        P("tp"),
        P("tp", None),
        P(None, "tp"),
        P("tp"),
        P(None, "tp"),
        P("tp"),
        P(None, "req", None, "tp"),
        P(None, "req", None, "tp"),
        P(),
        P(),
        P("req"),
        P("req"),
    )
    return jax.shard_map(
        functools.partial(local, mesh.shape["tp"]),
        mesh=mesh,
        in_specs=placed,
        out_specs=(P("req", "tp"), P(None, "req", None, "tp"), P(None, "req", None, "tp")),
        check_vma=False,
    )
```

```python
import functools

import jax
import jax.numpy as jnp
from jax import lax
from jax.experimental import pallas as pl
from jax.experimental.pallas import tpu as pltpu
from jax.sharding import PartitionSpec as P

STATE = 16
CONV = 4
RANK = 256
HALO = 16
WIDE = 1024
LANES = 128
SUBLANES = 8
LOG2E = 1.4426950408889634
F32 = jnp.float32
BF16 = jnp.bfloat16
HALF = 64
EDGE_AT = 8
NEXT_AT = 11
CHUNK = 16
FETCHES = 6
GROUPS_AT_ONCE = 4
PAIRS = 2
VMEM_LIMIT = 60 * 1024 * 1024
SMALL_LIMIT = 24 * 1024 * 1024


def low_half():
    return lax.broadcasted_iota(jnp.int32, (1, LANES), 1) < HALF


def silu(v):
    half = 0.5 * v
    return half + half * jnp.tanh(half)


def pack_kernel(length_ref, read_ref, store_ref, edge_ref, x_ref, out_ref, tiles_scr, low_scr, rows_scr, sem):
    n_req = read_ref.shape[1]
    slots = store_ref.shape[1]
    edge_rows = CONV - 1
    last = length_ref[0] - edge_rows
    first = pl.multiple_of(jnp.minimum(last // HALO * HALO, x_ref.shape[0] - 2 * HALO), HALO)
    copy = pltpu.make_async_copy(x_ref.at[pl.ds(first, 2 * HALO), :], low_scr, sem)
    copy.start()
    reads = (lax.broadcasted_iota(jnp.int32, (slots, n_req), 0) == read_ref[...]).astype(BF16)
    for row in range(STATE // 2):
        held = lax.dot_general(
            reads, store_ref[row * LANES : (row + 1) * LANES, :].astype(BF16), (((0,), (1,)), ((), ())),
            preferred_element_type=F32,
        )
        tiles_scr[pl.ds(row, n_req, stride=CHUNK), :] = held
    for row in range(edge_rows):
        edge = edge_ref[row * HALF : (row + 1) * HALF, :]
        held = lax.dot_general(
            reads, jnp.concatenate([edge, edge], axis=0), (((0,), (1,)), ((), ())), preferred_element_type=F32
        )
        tiles_scr[pl.ds(EDGE_AT + row, n_req, stride=CHUNK), :] = held
    for row in range(NEXT_AT + edge_rows, CHUNK):
        tiles_scr[pl.ds(row, n_req, stride=CHUNK), :] = jnp.zeros((n_req, LANES), F32)
    copy.wait()
    rows_scr[...] = low_scr[...].astype(F32)
    for row in range(edge_rows):
        line = rows_scr[pl.ds(last - first + row, 1), :]
        for req in range(n_req):
            at = req // 2 * LANES
            tiles_scr[req * CHUNK + NEXT_AT + row : req * CHUNK + NEXT_AT + row + 1, :] = line[:, at : at + LANES]
    out_ref[...] = tiles_scr[...].astype(BF16).reshape(out_ref.shape)


def pack(length, read_slot, store, edges, x):
    n_req = read_slot.shape[0]
    channels = x.shape[1]
    whole = lambda *_: (0, 0)
    return pl.pallas_call(
        pack_kernel,
        grid_spec=pltpu.PrefetchScalarGridSpec(
            num_scalar_prefetch=1,
            grid=(1,),
            in_specs=[
                pl.BlockSpec((1, n_req), whole),
                pl.BlockSpec(store.shape, whole),
                pl.BlockSpec(edges.shape, whole),
                pl.BlockSpec(memory_space=pl.ANY),
            ],
            out_specs=pl.BlockSpec((n_req, CHUNK, LANES), lambda *_: (0, 0, 0)),
            scratch_shapes=[
                pltpu.VMEM((n_req * CHUNK, LANES), F32),
                pltpu.VMEM((2 * HALO, channels), BF16),
                pltpu.VMEM((2 * HALO, channels), F32),
                pltpu.SemaphoreType.DMA,
            ],
        ),
        out_shape=jax.ShapeDtypeStruct((n_req, CHUNK, LANES), BF16),
        compiler_params=pltpu.CompilerParams(vmem_limit_bytes=VMEM_LIMIT),
        name="pack",
    )(length, read_slot.reshape(1, n_req), store, edges, x)


def conv_block(prev, x_ref, weight_ref, bias_ref, select_hbm, mixed_ref, part_ref, send, rows_scr, select_ref, sems):
    rows = x_ref.shape[0]
    groups = x_ref.shape[1] // LANES
    is_first = pl.program_id(0) == 0
    height = select_ref.shape[0] // FETCHES
    copies = [
        pltpu.make_async_copy(
            select_hbm.at[k * height : (k + 1) * height, :], select_ref.at[k * height : (k + 1) * height, :], sems.at[k]
        )
        for k in range(FETCHES)
    ]

    @pl.when(is_first)
    def _():
        for copy in copies:
            copy.start()

    def some_groups(step, _):
        for k in range(GROUPS_AT_ONCE):
            group = step * GROUPS_AT_ONCE + k
            at = pl.ds(pl.multiple_of(group * LANES, LANES), LANES)
            scr = rows_scr.at[k]
            scr[0:HALO, :] = prev(group)
            scr[HALO : HALO + rows, :] = x_ref[:, at].astype(F32)
            total = bias_ref[:, at] + weight_ref[CONV - 1 : CONV, at] * scr[HALO : HALO + rows, :]
            for tap in range(CONV - 1):
                first = HALO - (CONV - 1) + tap
                total = total + weight_ref[tap : tap + 1, at] * scr[first : first + rows, :]
            mixed_ref[:, at] = silu(total).astype(BF16)
        return 0

    lax.fori_loop(0, groups // GROUPS_AT_ONCE, some_groups, 0)

    @pl.when(is_first)
    def _():
        for copy in copies:
            copy.wait()

    part = lax.dot_general(
        select_ref[...], mixed_ref[...], (((1,), (1,)), ((), ())), preferred_element_type=F32
    ).T
    part_ref[...] = part
    send(part.astype(BF16))


def late_kernel(
    prev_ref, x_ref, weight_ref, bias_ref, select_ref, mixed_ref, part_ref, upper_ref, lower_ref, *scr, per_half
):
    prev = lambda group: prev_ref[:, pl.ds(pl.multiple_of(group * LANES, LANES), LANES)].astype(F32)
    block = 1 + pl.program_id(0)

    def send(part):
        @pl.when(block < per_half)
        def _():
            upper_ref[...] = part

        @pl.when(block >= per_half)
        def _():
            lower_ref[...] = part

    conv_block(prev, x_ref, weight_ref, bias_ref, select_ref, mixed_ref, part_ref, send, *scr)


def early_kernel(
    hit_ref, arrived_ref, x_ref, weight_ref, bias_ref, select_ref, late_mixed, late_part, late_upper,
    mixed_ref, part_ref, upper_ref, start_ref, tiles_scr, edge_scr, *scr
):
    del late_mixed, late_part, late_upper
    hit = hit_ref[0] > 0
    n_req = arrived_ref.shape[0]
    pairs = n_req // 2
    tiles = arrived_ref[...].astype(F32).reshape(n_req * CHUNK, LANES)
    tiles_scr[...] = jnp.where(hit, tiles, 0.0)
    low = low_half()
    even = lambda row: tiles_scr[pl.ds(row, pairs, stride=2 * CHUNK), :]
    odd = lambda row: tiles_scr[pl.ds(CHUNK + row, pairs, stride=2 * CHUNK), :]
    for row in range(STATE // 2):
        a, b = even(row), odd(row)
        first, second = jnp.where(low, a, pltpu.roll(b, HALF, 1)), jnp.where(low, pltpu.roll(a, HALF, 1), b)
        for block in range(pairs // SUBLANES):
            at = slice(block * SUBLANES, (block + 1) * SUBLANES)
            start_ref[block, 2 * row] = first[at]
            start_ref[block, 2 * row + 1] = second[at]
    edge_scr[...] = jnp.zeros(edge_scr.shape, F32)
    for row in range(CONV - 1):
        edge_scr[pl.ds(HALO - (CONV - 1) + row, pairs, stride=HALO), :] = jnp.where(low, even(EDGE_AT + row), odd(EDGE_AT + row))
    prev = lambda group: edge_scr[pl.ds(pl.multiple_of(group * HALO, HALO), HALO), :]

    def send(part):
        upper_ref[...] = part

    conv_block(prev, x_ref, weight_ref, bias_ref, select_ref, mixed_ref, part_ref, send, *scr)


def conv_rows(x, weight, bias, select_t, block, arrived=None, hit=None, late=None):
    rows, channels = x.shape
    wide = select_t.shape[0]
    first = 1 if late is None else 0
    steps = rows // block - 1 if late is None else 1
    per_half = rows // block // 2
    fixed = lambda *_: (0, 0)
    at = lambda i, *_: (first + i, 0)
    in_specs = [
        pl.BlockSpec((block, channels), at),
        pl.BlockSpec((CONV, channels), fixed),
        pl.BlockSpec((1, channels), fixed),
        pl.BlockSpec(memory_space=pl.ANY),
    ]
    upper_at = lambda i, *_: (jnp.minimum(first + i, per_half - 1), 0)
    lower_at = lambda i, *_: (jnp.maximum(first + i - per_half, 0), 0)
    out_specs = [
        pl.BlockSpec((block, channels), at),
        pl.BlockSpec((block, wide), at),
        pl.BlockSpec((block, wide), upper_at),
    ]
    out_shape = [
        jax.ShapeDtypeStruct((rows, channels), BF16),
        jax.ShapeDtypeStruct((rows, wide), F32),
        jax.ShapeDtypeStruct((rows // 2, wide), BF16),
    ]
    scratch = [
        pltpu.VMEM((GROUPS_AT_ONCE, HALO + block, LANES), F32),
        pltpu.VMEM(select_t.shape, BF16),
        pltpu.SemaphoreType.DMA((FETCHES,)),
    ]
    operands = [x, weight, bias, select_t]
    aliases = {}
    if late is None:
        kernel, name, scalars = functools.partial(late_kernel, per_half=per_half), "conv_late", []
        in_specs = [
            pl.BlockSpec((HALO, channels), lambda i, *_: ((first + i) * (block // HALO) - 1, 0))
        ] + in_specs
        operands = [x] + operands
        out_specs.append(pl.BlockSpec((block, wide), lower_at))
        out_shape.append(jax.ShapeDtypeStruct((rows // 2, wide), BF16))
    else:
        kernel, name, scalars = early_kernel, "conv_early", [hit]
        n_req = arrived.shape[0]
        in_specs = (
            [pl.BlockSpec(arrived.shape, lambda *_: (0, 0, 0))] + in_specs + [pl.BlockSpec(memory_space=pl.ANY)] * 3
        )
        operands = [arrived] + operands + list(late)
        aliases = {6: 0, 7: 1, 8: 2}
        start_shape = (channels // WIDE, STATE, SUBLANES, LANES)
        out_specs.append(pl.BlockSpec(start_shape, lambda *_: (0, 0, 0, 0)))
        out_shape.append(jax.ShapeDtypeStruct(start_shape, F32))
        scratch = [
            pltpu.VMEM((n_req * CHUNK, LANES), F32),
            pltpu.VMEM((channels // LANES * HALO, LANES), F32),
        ] + scratch
    return pl.pallas_call(
        kernel,
        grid_spec=pltpu.PrefetchScalarGridSpec(
            num_scalar_prefetch=len(scalars),
            grid=(steps,),
            in_specs=in_specs,
            out_specs=out_specs,
            scratch_shapes=scratch,
        ),
        out_shape=out_shape,
        input_output_aliases=aliases,
        compiler_params=pltpu.CompilerParams(vmem_limit_bytes=VMEM_LIMIT),
        cost_estimate=pl.CostEstimate(
            flops=2 * steps * block * channels * wide,
            bytes_accessed=steps * block * channels * 24,
            transcendentals=2 * steps * block * channels,
        ),
        name=name,
    )(*scalars, *operands)


def scan_kernel(length_ref, *refs):
    part_refs, refs = refs[:4], refs[4:]
    step_ref, bias_ref, decay_ref, skip_ref, mixed_ref, gate_ref, start_ref, *refs = refs
    out_ref, end_ref, norm_scr, wide_scr, value_scr, state_scr, rate_scr, back_scr, *lines = refs
    sizes, drives, scans = lines[0:2], lines[2:4], lines[4:6]
    rows = mixed_ref.shape[0]
    pairs = rows // HALO

    @pl.when(pl.program_id(0) == 0)
    def _():
        shape = (4 * STATE, 2 * STATE * LANES)
        source = lax.broadcasted_iota(jnp.int32, shape, 0) % (2 * STATE)
        spread = (source == lax.broadcasted_iota(jnp.int32, shape, 1) // LANES).astype(BF16)
        for half in range(2):
            sum_ref, more_ref = part_refs[2 * half : 2 * half + 2]
            for first in range(0, rows // 2, LANES):
                here = slice(first, first + LANES)
                there = slice(half * rows // 2 + first, half * rows // 2 + first + LANES)
                projected = sum_ref[here, :] + more_ref[here, :].astype(F32)
                low = projected[:, :RANK]
                scale = lax.rsqrt(jnp.mean(low * low, axis=-1, keepdims=True) + 1e-06)
                norm_scr[there, :] = (low * scale).astype(BF16)
                picks = projected[:, RANK:]
                high = picks.astype(BF16)
                both = jnp.concatenate([high, (picks - high.astype(F32)).astype(BF16)], axis=1)
                wide_scr[there, :] = jnp.dot(both, spread, preferred_element_type=F32)

    state_scr[...] = start_ref[0]
    rate = -jnp.exp(decay_ref[...]) * LOG2E
    for sub in range(SUBLANES):
        rate_scr[pl.ds(sub, STATE, stride=SUBLANES), :] = rate[:, sub * LANES : (sub + 1) * LANES]
    for first in range(0, rows, LANES):
        here = slice(first, first + LANES)
        value_scr[here, :] = jnp.dot(norm_scr[here, :], step_ref[...], preferred_element_type=F32)
    rates = [rate_scr[n * SUBLANES : (n + 1) * SUBLANES, :] for n in range(STATE)]
    row_in_tile = lax.broadcasted_iota(jnp.int32, (SUBLANES, LANES), 0)
    left = length_ref[0]

    def steps_of(pair, tile):
        first = pl.multiple_of(pair * HALO, HALO)
        live = row_in_tile < left - first - tile * SUBLANES
        for sub in range(SUBLANES):
            at = slice(sub * LANES, (sub + 1) * LANES)
            value = value_scr[pl.ds(first + tile * SUBLANES, SUBLANES), at] + bias_ref[:, at]
            small = jnp.exp2(jnp.abs(value) * -LOG2E)
            soft = jnp.where(small < 4e-3, small - 0.5 * small * small, jnp.log(1.0 + small))
            size = jnp.where(live, jnp.maximum(value, 0.0) + soft, 0.0)
            mixed = mixed_ref[pl.ds(first, HALO), at].astype(F32)[tile * SUBLANES : (tile + 1) * SUBLANES]
            sizes[tile][pl.ds(sub, SUBLANES, stride=SUBLANES), :] = size
            drives[tile][pl.ds(sub, SUBLANES, stride=SUBLANES), :] = size * mixed

    def advance(state, pair, tile):
        state = list(state)
        first = pl.multiple_of(pair * HALO + tile * SUBLANES, SUBLANES)
        picks = wide_scr.at[pl.ds(first, SUBLANES), :]
        for position in range(SUBLANES):
            here = slice(position * SUBLANES, (position + 1) * SUBLANES)
            size_row, drive_row = sizes[tile][here, :], drives[tile][here, :]
            sums = [None, None]
            for n in range(STATE):
                b = jnp.broadcast_to(picks[position : position + 1, n * LANES : (n + 1) * LANES], (SUBLANES, LANES))
                m = STATE + n
                c = jnp.broadcast_to(picks[position : position + 1, m * LANES : (m + 1) * LANES], (SUBLANES, LANES))
                state[n] = jnp.exp2(size_row * rates[n]) * state[n] + b * drive_row
                term = c * state[n]
                sums[n % 2] = term if sums[n % 2] is None else sums[n % 2] + term
            scans[tile][here, :] = sums[0] + sums[1]
        return tuple(state)

    def gate_of(pair):
        first = pl.multiple_of(pair * HALO, HALO)
        here = pl.ds(first, HALO)
        for sub in range(SUBLANES):
            at = slice(sub * LANES, (sub + 1) * LANES)
            scanned = jnp.concatenate(
                [scans[tile][pl.ds(sub, SUBLANES, stride=SUBLANES), :] for tile in range(2)], axis=0
            )
            value = scanned + skip_ref[:, at] * mixed_ref[here, at].astype(F32)
            value = value * silu(gate_ref[here, at].astype(F32))
            live = jnp.concatenate([row_in_tile, row_in_tile + SUBLANES], axis=0) < left - first
            out_ref[here, at] = jnp.where(live, value, 0.0).astype(BF16)

    def one_pair(pair, state):
        gate_of(jnp.maximum(pair - 1, 0))
        steps_of(pair, 1)
        state = advance(state, pair, 0)
        steps_of(jnp.minimum(pair + 1, pairs - 1), 0)
        return advance(state, pair, 1)

    def some_pairs(step, state):
        for k in range(PAIRS):
            state = one_pair(step * PAIRS + k, state)
        return state

    steps_of(0, 0)
    state = lax.fori_loop(0, pairs // PAIRS, some_pairs, tuple(state_scr[n] for n in range(STATE)))
    gate_of(pairs - 1)

    low = low_half()
    for row in range(STATE // 2):
        a, b = state[2 * row], state[2 * row + 1]
        even = jnp.where(low, a, pltpu.roll(b, HALF, 1))
        odd = jnp.where(low, pltpu.roll(a, HALF, 1), b)
        back_scr[pl.ds(row, SUBLANES, stride=2 * SUBLANES), :] = even
        back_scr[pl.ds(SUBLANES + row, SUBLANES, stride=2 * SUBLANES), :] = odd
    end_ref[...] = back_scr[...].astype(BF16).reshape(end_ref.shape)


def scan_rows(length, parts, step_weight, step_bias, decay_log, skip_gain, mixed, gate, start):
    rows, channels = mixed.shape
    blocks = channels // WIDE
    by_channel = lambda c, *_: (0, c)
    per_block = WIDE // HALF
    return pl.pallas_call(
        scan_kernel,
        grid_spec=pltpu.PrefetchScalarGridSpec(
            num_scalar_prefetch=1,
            grid=(blocks,),
            in_specs=[pl.BlockSpec(part.shape, lambda c, *_: (0, 0)) for part in parts]
            + [
                pl.BlockSpec((RANK, WIDE), by_channel),
                pl.BlockSpec((1, WIDE), by_channel),
                pl.BlockSpec((STATE, WIDE), by_channel),
                pl.BlockSpec((1, WIDE), by_channel),
                pl.BlockSpec((rows, WIDE), by_channel),
                pl.BlockSpec((rows, WIDE), by_channel),
                pl.BlockSpec((1, STATE, SUBLANES, LANES), lambda c, *_: (c, 0, 0, 0)),
            ],
            out_specs=[
                pl.BlockSpec((rows, WIDE), by_channel),
                pl.BlockSpec((per_block, SUBLANES, LANES), lambda c, *_: (c, 0, 0)),
            ],
            scratch_shapes=[
                pltpu.VMEM((rows, RANK), BF16),
                pltpu.VMEM((rows, 2 * STATE * LANES), F32),
                pltpu.VMEM((rows, WIDE), F32),
                pltpu.VMEM((STATE, SUBLANES, LANES), F32),
                pltpu.VMEM((STATE * SUBLANES, LANES), F32),
                pltpu.VMEM((per_block * SUBLANES, LANES), F32),
            ]
            + [pltpu.VMEM((SUBLANES * SUBLANES, LANES), F32)] * 6,
        ),
        out_shape=[
            jax.ShapeDtypeStruct(gate.shape, BF16),
            jax.ShapeDtypeStruct((blocks * per_block, SUBLANES, LANES), BF16),
        ],
        compiler_params=pltpu.CompilerParams(vmem_limit_bytes=VMEM_LIMIT),
        cost_estimate=pl.CostEstimate(
            flops=2 * rows * channels * RANK + 100 * rows * channels * STATE,
            bytes_accessed=rows * channels * 8,
            transcendentals=rows * channels * STATE,
        ),
        name="scan_rows",
    )(length, *parts, step_weight, step_bias, decay_log, skip_gain, mixed, gate, start)


def save_kernel(slot_ref, half_ref, tiles_ref, store_ref, out_ref, tiles_scr, *, n_rows, first_row, halves):
    n_req, chunk, _ = tiles_ref.shape
    slots = store_ref.shape[1]
    saves = slot_ref[...] == lax.broadcasted_iota(jnp.int32, (n_req, slots), 1)
    saved = jnp.max(saves.astype(F32), axis=0, keepdims=True) > 0.0
    saves = saves.astype(BF16)
    tiles = tiles_ref[...].astype(F32).reshape(n_req * chunk, LANES)
    if halves:
        tiles = jnp.where(half_ref[0] > 0, pltpu.roll(tiles, HALF, 1), tiles)
    tiles_scr[...] = tiles
    height = HALF if halves else LANES
    for row in range(n_rows):
        new = tiles_scr[pl.ds(first_row + row, n_req, stride=chunk), :].astype(BF16)
        new = lax.dot_general(new, saves, (((0,), (0,)), ((), ())), preferred_element_type=F32)[:height]
        at = slice(row * height, (row + 1) * height)
        out_ref[at, :] = jnp.where(saved, new, store_ref[at, :].astype(F32)).astype(out_ref.dtype)


def save(save_slot, half, tiles, store, n_rows, first_row, halves):
    n_req, chunk, _ = tiles.shape
    whole = lambda *_: (0, 0)
    return pl.pallas_call(
        functools.partial(save_kernel, n_rows=n_rows, first_row=first_row, halves=halves),
        grid=(1,),
        in_specs=[
            pl.BlockSpec((n_req, 1), whole),
            pl.BlockSpec(memory_space=pltpu.SMEM),
            pl.BlockSpec(tiles.shape, lambda *_: (0, 0, 0)),
            pl.BlockSpec(store.shape, whole),
        ],
        out_specs=pl.BlockSpec(store.shape, whole),
        out_shape=jax.ShapeDtypeStruct(store.shape, store.dtype),
        scratch_shapes=[pltpu.VMEM((n_req * chunk, LANES), F32)],
        compiler_params=pltpu.CompilerParams(vmem_limit_bytes=SMALL_LIMIT),
        name="save",
    )(save_slot.reshape(n_req, 1), half, tiles, store)


def pairwise(part, sent, n_tp):
    rows = sent[0].shape[0]
    inner = [(d, d ^ 1) for d in range(n_tp)]
    outer = [(d, n_tp - 1 - d) for d in range(n_tp)]
    orders = ((inner, outer), (outer, inner))
    got = [lax.ppermute(half, "tp", order[0]) for half, order in zip(sent, orders)]
    sums = [part[k * rows : (k + 1) * rows] + got[k].astype(F32) for k in range(2)]
    more = [lax.ppermute(total.astype(BF16), "tp", order[1]) for total, order in zip(sums, orders)]
    return [sums[0], more[0], sums[1], more[1]]


def local(
    n_tp,
    conv_input,
    gate_input,
    conv_weight,
    conv_bias,
    select_weight,
    step_weight,
    step_bias,
    decay_log,
    skip_gain,
    store_state,
    store_edge,
    read_slot,
    save_slot,
    cache_hit,
    suffix_length,
):
    local_rows, channels = conv_input.shape
    slots, _, _, stripe = store_state.shape
    edge_rows = CONV - 1
    store = store_state.transpose(1, 2, 3, 0).reshape(STATE * stripe, slots)
    edges = store_edge.transpose(1, 2, 3, 0).reshape(edge_rows * stripe, slots)
    outgoing = pack(suffix_length, read_slot, store, edges, conv_input)
    arrived = lax.all_to_all(outgoing, "req", split_axis=0, concat_axis=0, tiled=True)

    select_t = select_weight.T
    conv_bias = conv_bias.reshape(1, channels)
    step_bias = step_bias.reshape(1, channels)
    skip_gain = skip_gain.reshape(1, channels)
    block = local_rows // 4
    conv = functools.partial(conv_rows, conv_input, conv_weight, conv_bias, select_t, block)
    *late, lower = conv()
    mixed, part, upper, start = conv(arrived, cache_hit, late)
    half = (lax.axis_index("req") % 2).astype(jnp.int32).reshape(1)
    new_edges = save(save_slot, half, arrived, edges, edge_rows, NEXT_AT, True)
    parts = pairwise(part, (upper, lower), n_tp)
    new_edges, *parts = lax.optimization_barrier((new_edges, *parts))
    out, back = scan_rows(
        suffix_length, parts, step_weight, step_bias, decay_log, skip_gain, mixed, gate_input, start
    )
    back = lax.all_to_all(back, "req", split_axis=0, concat_axis=0, tiled=True)
    new_store = save(save_slot, half, back, store, STATE // 2, 0, False)
    new_state = new_store.reshape(1, STATE, stripe, slots).transpose(3, 0, 1, 2)
    new_edge_store = new_edges.reshape(1, edge_rows, stripe, slots).transpose(3, 0, 1, 2)
    return (out, new_state, new_edge_store)


def solution(mesh):
    placed = (
        P("req", "tp"),
        P("req", "tp"),
        P(None, "tp"),
        P("tp"),
        P("tp", None),
        P(None, "tp"),
        P("tp"),
        P(None, "tp"),
        P("tp"),
        P(None, "req", None, "tp"),
        P(None, "req", None, "tp"),
        P(),
        P(),
        P("req"),
        P("req"),
    )
    return jax.shard_map(
        functools.partial(local, mesh.shape["tp"]),
        mesh=mesh,
        in_specs=placed,
        out_specs=(P("req", "tp"), P(None, "req", None, "tp"), P(None, "req", None, "tp")),
        check_vma=False,
    )
```

```python
import functools

import jax
import jax.numpy as jnp
from jax import lax
from jax.experimental import pallas as pl
from jax.experimental.pallas import tpu as pltpu
from jax.sharding import PartitionSpec as P

STATE = 16
CONV = 4
RANK = 256
HALO = 16
WIDE = 1024
LANES = 128
SUBLANES = 8
LOG2E = 1.4426950408889634
F32 = jnp.float32
BF16 = jnp.bfloat16
HALF = 64
EDGE_AT = 8
NEXT_AT = 11
CHUNK = 16
FETCHES = 6
GROUPS_AT_ONCE = 4
PAIRS = 2
VMEM_LIMIT = 60 * 1024 * 1024
SMALL_LIMIT = 24 * 1024 * 1024


def low_half():
    return lax.broadcasted_iota(jnp.int32, (1, LANES), 1) < HALF


def silu(v):
    half = 0.5 * v
    return half + half * jnp.tanh(half)


def pack_kernel(length_ref, read_ref, store_ref, edge_ref, x_ref, out_ref, tiles_scr, low_scr, rows_scr, sem):
    n_req = read_ref.shape[1]
    slots = store_ref.shape[1]
    edge_rows = CONV - 1
    last = length_ref[0] - edge_rows
    first = pl.multiple_of(jnp.minimum(last // HALO * HALO, x_ref.shape[0] - 2 * HALO), HALO)
    copy = pltpu.make_async_copy(x_ref.at[pl.ds(first, 2 * HALO), :], low_scr, sem)
    copy.start()
    reads = (lax.broadcasted_iota(jnp.int32, (slots, n_req), 0) == read_ref[...]).astype(BF16)
    for row in range(STATE // 2):
        held = lax.dot_general(
            reads, store_ref[row * LANES : (row + 1) * LANES, :].astype(BF16), (((0,), (1,)), ((), ())),
            preferred_element_type=F32,
        )
        tiles_scr[pl.ds(row, n_req, stride=CHUNK), :] = held
    for row in range(edge_rows):
        edge = edge_ref[row * HALF : (row + 1) * HALF, :]
        held = lax.dot_general(
            reads, jnp.concatenate([edge, edge], axis=0), (((0,), (1,)), ((), ())), preferred_element_type=F32
        )
        tiles_scr[pl.ds(EDGE_AT + row, n_req, stride=CHUNK), :] = held
    for row in range(NEXT_AT + edge_rows, CHUNK):
        tiles_scr[pl.ds(row, n_req, stride=CHUNK), :] = jnp.zeros((n_req, LANES), F32)
    copy.wait()
    rows_scr[...] = low_scr[...].astype(F32)
    for row in range(edge_rows):
        line = rows_scr[pl.ds(last - first + row, 1), :]
        for req in range(n_req):
            at = req // 2 * LANES
            tiles_scr[req * CHUNK + NEXT_AT + row : req * CHUNK + NEXT_AT + row + 1, :] = line[:, at : at + LANES]
    out_ref[...] = tiles_scr[...].astype(BF16).reshape(out_ref.shape)


def pack(length, read_slot, store, edges, x):
    n_req = read_slot.shape[0]
    channels = x.shape[1]
    whole = lambda *_: (0, 0)
    return pl.pallas_call(
        pack_kernel,
        grid_spec=pltpu.PrefetchScalarGridSpec(
            num_scalar_prefetch=1,
            grid=(1,),
            in_specs=[
                pl.BlockSpec((1, n_req), whole),
                pl.BlockSpec(store.shape, whole),
                pl.BlockSpec(edges.shape, whole),
                pl.BlockSpec(memory_space=pl.ANY),
            ],
            out_specs=pl.BlockSpec((n_req, CHUNK, LANES), lambda *_: (0, 0, 0)),
            scratch_shapes=[
                pltpu.VMEM((n_req * CHUNK, LANES), F32),
                pltpu.VMEM((2 * HALO, channels), BF16),
                pltpu.VMEM((2 * HALO, channels), F32),
                pltpu.SemaphoreType.DMA,
            ],
        ),
        out_shape=jax.ShapeDtypeStruct((n_req, CHUNK, LANES), BF16),
        compiler_params=pltpu.CompilerParams(vmem_limit_bytes=VMEM_LIMIT),
        name="pack",
    )(length, read_slot.reshape(1, n_req), store, edges, x)


def conv_block(prev, x_ref, weight_ref, bias_ref, select_hbm, mixed_ref, part_ref, send_ref, rows_scr, select_ref, sems):
    rows = x_ref.shape[0]
    groups = x_ref.shape[1] // LANES
    is_first = pl.program_id(0) == 0
    height = select_ref.shape[0] // FETCHES
    copies = [
        pltpu.make_async_copy(
            select_hbm.at[k * height : (k + 1) * height, :], select_ref.at[k * height : (k + 1) * height, :], sems.at[k]
        )
        for k in range(FETCHES)
    ]

    @pl.when(is_first)
    def _():
        for copy in copies:
            copy.start()

    def some_groups(step, _):
        for k in range(GROUPS_AT_ONCE):
            group = step * GROUPS_AT_ONCE + k
            at = pl.ds(pl.multiple_of(group * LANES, LANES), LANES)
            scr = rows_scr.at[k]
            scr[0:HALO, :] = prev(group)
            scr[HALO : HALO + rows, :] = x_ref[:, at].astype(F32)
            total = bias_ref[:, at] + weight_ref[CONV - 1 : CONV, at] * scr[HALO : HALO + rows, :]
            for tap in range(CONV - 1):
                first = HALO - (CONV - 1) + tap
                total = total + weight_ref[tap : tap + 1, at] * scr[first : first + rows, :]
            mixed_ref[:, at] = silu(total).astype(BF16)
        return 0

    lax.fori_loop(0, groups // GROUPS_AT_ONCE, some_groups, 0)

    @pl.when(is_first)
    def _():
        for copy in copies:
            copy.wait()

    part = lax.dot_general(
        select_ref[...], mixed_ref[...], (((1,), (1,)), ((), ())), preferred_element_type=F32
    ).T
    part_ref[...] = part
    send_ref[...] = part.astype(BF16)


def late_kernel(prev_ref, x_ref, weight_ref, bias_ref, select_ref, mixed_ref, part_ref, send_ref, *scr):
    prev = lambda group: prev_ref[:, pl.ds(pl.multiple_of(group * LANES, LANES), LANES)].astype(F32)
    conv_block(prev, x_ref, weight_ref, bias_ref, select_ref, mixed_ref, part_ref, send_ref, *scr)


def early_kernel(
    hit_ref, arrived_ref, x_ref, weight_ref, bias_ref, select_ref, late_ref, mixed_ref, part_ref, send_ref, start_ref,
    tiles_scr, edge_scr, *scr
):
    del late_ref
    hit = hit_ref[0] > 0
    n_req = arrived_ref.shape[0]
    pairs = n_req // 2
    tiles = arrived_ref[...].astype(F32).reshape(n_req * CHUNK, LANES)
    tiles_scr[...] = jnp.where(hit, tiles, 0.0)
    low = low_half()
    even = lambda row: tiles_scr[pl.ds(row, pairs, stride=2 * CHUNK), :]
    odd = lambda row: tiles_scr[pl.ds(CHUNK + row, pairs, stride=2 * CHUNK), :]
    for row in range(STATE // 2):
        a, b = even(row), odd(row)
        first, second = jnp.where(low, a, pltpu.roll(b, HALF, 1)), jnp.where(low, pltpu.roll(a, HALF, 1), b)
        for block in range(pairs // SUBLANES):
            at = slice(block * SUBLANES, (block + 1) * SUBLANES)
            start_ref[block, 2 * row] = first[at]
            start_ref[block, 2 * row + 1] = second[at]
    edge_scr[...] = jnp.zeros(edge_scr.shape, F32)
    for row in range(CONV - 1):
        edge_scr[pl.ds(HALO - (CONV - 1) + row, pairs, stride=HALO), :] = jnp.where(low, even(EDGE_AT + row), odd(EDGE_AT + row))
    prev = lambda group: edge_scr[pl.ds(pl.multiple_of(group * HALO, HALO), HALO), :]
    conv_block(prev, x_ref, weight_ref, bias_ref, select_ref, mixed_ref, part_ref, send_ref, *scr)


def conv_rows(x, weight, bias, select_t, block, arrived=None, hit=None, late=None):
    rows, channels = x.shape
    wide = select_t.shape[0]
    first = 1 if late is None else 0
    steps = rows // block - 1 if late is None else 1
    fixed = lambda *_: (0, 0)
    at = lambda i, *_: (first + i, 0)
    in_specs = [
        pl.BlockSpec((block, channels), at),
        pl.BlockSpec((CONV, channels), fixed),
        pl.BlockSpec((1, channels), fixed),
        pl.BlockSpec(memory_space=pl.ANY),
    ]
    out_specs = [pl.BlockSpec((block, channels), at)] + [pl.BlockSpec((block, wide), lambda i, *_: (i, 0))] * 2
    out_shape = [
        jax.ShapeDtypeStruct((rows, channels), BF16),
        jax.ShapeDtypeStruct((steps * block, wide), F32),
        jax.ShapeDtypeStruct((steps * block, wide), BF16),
    ]
    scratch = [
        pltpu.VMEM((GROUPS_AT_ONCE, HALO + block, LANES), F32),
        pltpu.VMEM(select_t.shape, BF16),
        pltpu.SemaphoreType.DMA((FETCHES,)),
    ]
    operands = [x, weight, bias, select_t]
    aliases = {}
    if late is None:
        kernel, name, scalars = late_kernel, "conv_late", []
        in_specs = [
            pl.BlockSpec((HALO, channels), lambda i, *_: ((first + i) * (block // HALO) - 1, 0))
        ] + in_specs
        operands = [x] + operands
    else:
        kernel, name, scalars = early_kernel, "conv_early", [hit]
        n_req = arrived.shape[0]
        in_specs = [pl.BlockSpec(arrived.shape, lambda *_: (0, 0, 0))] + in_specs + [pl.BlockSpec(memory_space=pl.ANY)]
        operands = [arrived] + operands + [late]
        aliases = {6: 0}
        start_shape = (channels // WIDE, STATE, SUBLANES, LANES)
        out_specs.append(pl.BlockSpec(start_shape, lambda *_: (0, 0, 0, 0)))
        out_shape.append(jax.ShapeDtypeStruct(start_shape, F32))
        scratch = [
            pltpu.VMEM((n_req * CHUNK, LANES), F32),
            pltpu.VMEM((channels // LANES * HALO, LANES), F32),
        ] + scratch
    return pl.pallas_call(
        kernel,
        grid_spec=pltpu.PrefetchScalarGridSpec(
            num_scalar_prefetch=len(scalars),
            grid=(steps,),
            in_specs=in_specs,
            out_specs=out_specs,
            scratch_shapes=scratch,
        ),
        out_shape=out_shape,
        input_output_aliases=aliases,
        compiler_params=pltpu.CompilerParams(vmem_limit_bytes=VMEM_LIMIT),
        cost_estimate=pl.CostEstimate(
            flops=2 * steps * block * channels * wide,
            bytes_accessed=steps * block * channels * 24,
            transcendentals=2 * steps * block * channels,
        ),
        name=name,
    )(*scalars, *operands)


def scan_kernel(length_ref, *refs):
    part_refs, refs = refs[:4], refs[4:]
    step_ref, bias_ref, decay_ref, skip_ref, mixed_ref, gate_ref, start_ref, *refs = refs
    out_ref, end_ref, norm_scr, wide_scr, value_scr, state_scr, rate_scr, back_scr, *lines = refs
    sizes, drives, scans = lines[0:2], lines[2:4], lines[4:6]
    rows = mixed_ref.shape[0]
    pairs = rows // HALO

    @pl.when(pl.program_id(0) == 0)
    def _():
        shape = (4 * STATE, 2 * STATE * LANES)
        source = lax.broadcasted_iota(jnp.int32, shape, 0) % (2 * STATE)
        spread = (source == lax.broadcasted_iota(jnp.int32, shape, 1) // LANES).astype(BF16)
        done = 0
        for sum_ref, more_ref in (part_refs[:2], part_refs[2:]):
            for first in range(0, sum_ref.shape[0], LANES):
                here = slice(first, first + LANES)
                there = slice(done, done + LANES)
                done += LANES
                projected = sum_ref[here, :] + more_ref[here, :].astype(F32)
                low = projected[:, :RANK]
                scale = lax.rsqrt(jnp.mean(low * low, axis=-1, keepdims=True) + 1e-06)
                norm_scr[there, :] = (low * scale).astype(BF16)
                picks = projected[:, RANK:]
                high = picks.astype(BF16)
                both = jnp.concatenate([high, (picks - high.astype(F32)).astype(BF16)], axis=1)
                wide_scr[there, :] = jnp.dot(both, spread, preferred_element_type=F32)

    state_scr[...] = start_ref[0]
    rate = -jnp.exp(decay_ref[...]) * LOG2E
    for sub in range(SUBLANES):
        rate_scr[pl.ds(sub, STATE, stride=SUBLANES), :] = rate[:, sub * LANES : (sub + 1) * LANES]
    for first in range(0, rows, LANES):
        here = slice(first, first + LANES)
        value_scr[here, :] = jnp.dot(norm_scr[here, :], step_ref[...], preferred_element_type=F32)
    rates = [rate_scr[n * SUBLANES : (n + 1) * SUBLANES, :] for n in range(STATE)]
    row_in_tile = lax.broadcasted_iota(jnp.int32, (SUBLANES, LANES), 0)
    left = length_ref[0]

    def steps_of(pair, tile):
        first = pl.multiple_of(pair * HALO, HALO)
        live = row_in_tile < left - first - tile * SUBLANES
        for sub in range(SUBLANES):
            at = slice(sub * LANES, (sub + 1) * LANES)
            value = value_scr[pl.ds(first + tile * SUBLANES, SUBLANES), at] + bias_ref[:, at]
            small = jnp.exp2(jnp.abs(value) * -LOG2E)
            soft = jnp.where(small < 4e-3, small - 0.5 * small * small, jnp.log(1.0 + small))
            size = jnp.where(live, jnp.maximum(value, 0.0) + soft, 0.0)
            mixed = mixed_ref[pl.ds(first, HALO), at].astype(F32)[tile * SUBLANES : (tile + 1) * SUBLANES]
            sizes[tile][pl.ds(sub, SUBLANES, stride=SUBLANES), :] = size
            drives[tile][pl.ds(sub, SUBLANES, stride=SUBLANES), :] = size * mixed

    def advance(state, pair, tile):
        state = list(state)
        first = pl.multiple_of(pair * HALO + tile * SUBLANES, SUBLANES)
        picks = wide_scr.at[pl.ds(first, SUBLANES), :]
        for position in range(SUBLANES):
            here = slice(position * SUBLANES, (position + 1) * SUBLANES)
            size_row, drive_row = sizes[tile][here, :], drives[tile][here, :]
            sums = [None, None]
            for n in range(STATE):
                b = jnp.broadcast_to(picks[position : position + 1, n * LANES : (n + 1) * LANES], (SUBLANES, LANES))
                m = STATE + n
                c = jnp.broadcast_to(picks[position : position + 1, m * LANES : (m + 1) * LANES], (SUBLANES, LANES))
                state[n] = jnp.exp2(size_row * rates[n]) * state[n] + b * drive_row
                term = c * state[n]
                sums[n % 2] = term if sums[n % 2] is None else sums[n % 2] + term
            scans[tile][here, :] = sums[0] + sums[1]
        return tuple(state)

    def gate_of(pair):
        first = pl.multiple_of(pair * HALO, HALO)
        here = pl.ds(first, HALO)
        for sub in range(SUBLANES):
            at = slice(sub * LANES, (sub + 1) * LANES)
            scanned = jnp.concatenate(
                [scans[tile][pl.ds(sub, SUBLANES, stride=SUBLANES), :] for tile in range(2)], axis=0
            )
            value = scanned + skip_ref[:, at] * mixed_ref[here, at].astype(F32)
            value = value * silu(gate_ref[here, at].astype(F32))
            live = jnp.concatenate([row_in_tile, row_in_tile + SUBLANES], axis=0) < left - first
            out_ref[here, at] = jnp.where(live, value, 0.0).astype(BF16)

    def one_pair(pair, state):
        gate_of(jnp.maximum(pair - 1, 0))
        steps_of(pair, 1)
        state = advance(state, pair, 0)
        steps_of(jnp.minimum(pair + 1, pairs - 1), 0)
        return advance(state, pair, 1)

    def some_pairs(step, state):
        for k in range(PAIRS):
            state = one_pair(step * PAIRS + k, state)
        return state

    steps_of(0, 0)
    state = lax.fori_loop(0, pairs // PAIRS, some_pairs, tuple(state_scr[n] for n in range(STATE)))
    gate_of(pairs - 1)

    low = low_half()
    for row in range(STATE // 2):
        a, b = state[2 * row], state[2 * row + 1]
        even = jnp.where(low, a, pltpu.roll(b, HALF, 1))
        odd = jnp.where(low, pltpu.roll(a, HALF, 1), b)
        back_scr[pl.ds(row, SUBLANES, stride=2 * SUBLANES), :] = even
        back_scr[pl.ds(SUBLANES + row, SUBLANES, stride=2 * SUBLANES), :] = odd
    end_ref[...] = back_scr[...].astype(BF16).reshape(end_ref.shape)


def scan_rows(length, parts, step_weight, step_bias, decay_log, skip_gain, mixed, gate, start):
    rows, channels = mixed.shape
    blocks = channels // WIDE
    by_channel = lambda c, *_: (0, c)
    per_block = WIDE // HALF
    return pl.pallas_call(
        scan_kernel,
        grid_spec=pltpu.PrefetchScalarGridSpec(
            num_scalar_prefetch=1,
            grid=(blocks,),
            in_specs=[pl.BlockSpec(part.shape, lambda c, *_: (0, 0)) for part in parts]
            + [
                pl.BlockSpec((RANK, WIDE), by_channel),
                pl.BlockSpec((1, WIDE), by_channel),
                pl.BlockSpec((STATE, WIDE), by_channel),
                pl.BlockSpec((1, WIDE), by_channel),
                pl.BlockSpec((rows, WIDE), by_channel),
                pl.BlockSpec((rows, WIDE), by_channel),
                pl.BlockSpec((1, STATE, SUBLANES, LANES), lambda c, *_: (c, 0, 0, 0)),
            ],
            out_specs=[
                pl.BlockSpec((rows, WIDE), by_channel),
                pl.BlockSpec((per_block, SUBLANES, LANES), lambda c, *_: (c, 0, 0)),
            ],
            scratch_shapes=[
                pltpu.VMEM((rows, RANK), BF16),
                pltpu.VMEM((rows, 2 * STATE * LANES), F32),
                pltpu.VMEM((rows, WIDE), F32),
                pltpu.VMEM((STATE, SUBLANES, LANES), F32),
                pltpu.VMEM((STATE * SUBLANES, LANES), F32),
                pltpu.VMEM((per_block * SUBLANES, LANES), F32),
            ]
            + [pltpu.VMEM((SUBLANES * SUBLANES, LANES), F32)] * 6,
        ),
        out_shape=[
            jax.ShapeDtypeStruct(gate.shape, BF16),
            jax.ShapeDtypeStruct((blocks * per_block, SUBLANES, LANES), BF16),
        ],
        compiler_params=pltpu.CompilerParams(vmem_limit_bytes=VMEM_LIMIT),
        cost_estimate=pl.CostEstimate(
            flops=2 * rows * channels * RANK + 100 * rows * channels * STATE,
            bytes_accessed=rows * channels * 8,
            transcendentals=rows * channels * STATE,
        ),
        name="scan_rows",
    )(length, *parts, step_weight, step_bias, decay_log, skip_gain, mixed, gate, start)


def save_kernel(slot_ref, half_ref, tiles_ref, store_ref, out_ref, tiles_scr, *, n_rows, first_row, halves):
    n_req, chunk, _ = tiles_ref.shape
    slots = store_ref.shape[1]
    saves = slot_ref[...] == lax.broadcasted_iota(jnp.int32, (n_req, slots), 1)
    saved = jnp.max(saves.astype(F32), axis=0, keepdims=True) > 0.0
    saves = saves.astype(BF16)
    tiles = tiles_ref[...].astype(F32).reshape(n_req * chunk, LANES)
    if halves:
        tiles = jnp.where(half_ref[0] > 0, pltpu.roll(tiles, HALF, 1), tiles)
    tiles_scr[...] = tiles
    height = HALF if halves else LANES
    for row in range(n_rows):
        new = tiles_scr[pl.ds(first_row + row, n_req, stride=chunk), :].astype(BF16)
        new = lax.dot_general(new, saves, (((0,), (0,)), ((), ())), preferred_element_type=F32)[:height]
        at = slice(row * height, (row + 1) * height)
        out_ref[at, :] = jnp.where(saved, new, store_ref[at, :].astype(F32)).astype(out_ref.dtype)


def save(save_slot, half, tiles, store, n_rows, first_row, halves):
    n_req, chunk, _ = tiles.shape
    whole = lambda *_: (0, 0)
    return pl.pallas_call(
        functools.partial(save_kernel, n_rows=n_rows, first_row=first_row, halves=halves),
        grid=(1,),
        in_specs=[
            pl.BlockSpec((n_req, 1), whole),
            pl.BlockSpec(memory_space=pltpu.SMEM),
            pl.BlockSpec(tiles.shape, lambda *_: (0, 0, 0)),
            pl.BlockSpec(store.shape, whole),
        ],
        out_specs=pl.BlockSpec(store.shape, whole),
        out_shape=jax.ShapeDtypeStruct(store.shape, store.dtype),
        scratch_shapes=[pltpu.VMEM((n_req * chunk, LANES), F32)],
        compiler_params=pltpu.CompilerParams(vmem_limit_bytes=SMALL_LIMIT),
        name="save",
    )(save_slot.reshape(n_req, 1), half, tiles, store)


def pairwise(part, sent, orders):
    total = part + lax.ppermute(sent, "tp", orders[0]).astype(F32)
    return [total, lax.ppermute(total.astype(BF16), "tp", orders[1])]


def local(
    n_tp,
    conv_input,
    gate_input,
    conv_weight,
    conv_bias,
    select_weight,
    step_weight,
    step_bias,
    decay_log,
    skip_gain,
    store_state,
    store_edge,
    read_slot,
    save_slot,
    cache_hit,
    suffix_length,
):
    local_rows, channels = conv_input.shape
    slots, _, _, stripe = store_state.shape
    edge_rows = CONV - 1
    store = store_state.transpose(1, 2, 3, 0).reshape(STATE * stripe, slots)
    edges = store_edge.transpose(1, 2, 3, 0).reshape(edge_rows * stripe, slots)
    outgoing = pack(suffix_length, read_slot, store, edges, conv_input)
    arrived = lax.all_to_all(outgoing, "req", split_axis=0, concat_axis=0, tiled=True)

    select_t = select_weight.T
    conv_bias = conv_bias.reshape(1, channels)
    step_bias = step_bias.reshape(1, channels)
    skip_gain = skip_gain.reshape(1, channels)
    block = local_rows // 4
    conv = functools.partial(conv_rows, conv_input, conv_weight, conv_bias, select_t, block)
    inner = [(d, d ^ 1) for d in range(n_tp)]
    outer = [(d, n_tp - 1 - d) for d in range(n_tp)]
    late, late_part, late_sent = conv()
    late_parts = pairwise(late_part, late_sent, (outer, inner))
    mixed, early_part, early_sent, start = conv(arrived, cache_hit, late)
    parts = pairwise(early_part, early_sent, (inner, outer)) + late_parts
    half = (lax.axis_index("req") % 2).astype(jnp.int32).reshape(1)
    new_edges = save(save_slot, half, arrived, edges, edge_rows, NEXT_AT, True)
    new_edges, *parts = lax.optimization_barrier((new_edges, *parts))
    out, back = scan_rows(
        suffix_length, parts, step_weight, step_bias, decay_log, skip_gain, mixed, gate_input, start
    )
    back = lax.all_to_all(back, "req", split_axis=0, concat_axis=0, tiled=True)
    new_store = save(save_slot, half, back, store, STATE // 2, 0, False)
    new_state = new_store.reshape(1, STATE, stripe, slots).transpose(3, 0, 1, 2)
    new_edge_store = new_edges.reshape(1, edge_rows, stripe, slots).transpose(3, 0, 1, 2)
    return (out, new_state, new_edge_store)


def solution(mesh):
    placed = (
        P("req", "tp"),
        P("req", "tp"),
        P(None, "tp"),
        P("tp"),
        P("tp", None),
        P(None, "tp"),
        P("tp"),
        P(None, "tp"),
        P("tp"),
        P(None, "req", None, "tp"),
        P(None, "req", None, "tp"),
        P(),
        P(),
        P("req"),
        P("req"),
    )
    return jax.shard_map(
        functools.partial(local, mesh.shape["tp"]),
        mesh=mesh,
        in_specs=placed,
        out_specs=(P("req", "tp"), P(None, "req", None, "tp"), P(None, "req", None, "tp")),
        check_vma=False,
    )
```

```python
import functools

import jax
import jax.numpy as jnp
from jax import lax
from jax.experimental import pallas as pl
from jax.experimental.pallas import tpu as pltpu
from jax.sharding import PartitionSpec as P

STATE = 16
CONV = 4
RANK = 256
HALO = 16
WIDE = 1024
LANES = 128
SUBLANES = 8
LOG2E = 1.4426950408889634
F32 = jnp.float32
BF16 = jnp.bfloat16
HALF = 64
EDGE_AT = 8
NEXT_AT = 11
CHUNK = 16
FETCHES = 6
GROUPS_AT_ONCE = 4
PAIRS = 2
EARLY_PARTS = 4
VMEM_LIMIT = 60 * 1024 * 1024
SMALL_LIMIT = 24 * 1024 * 1024


def low_half():
    return lax.broadcasted_iota(jnp.int32, (1, LANES), 1) < HALF


def silu(v):
    half = 0.5 * v
    return half + half * jnp.tanh(half)


def pack_kernel(length_ref, read_ref, store_ref, edge_ref, x_ref, out_ref, tiles_scr, low_scr, rows_scr, sem):
    n_req = read_ref.shape[1]
    slots = store_ref.shape[1]
    edge_rows = CONV - 1
    last = length_ref[0] - edge_rows
    first = pl.multiple_of(jnp.minimum(last // HALO * HALO, x_ref.shape[0] - 2 * HALO), HALO)
    copy = pltpu.make_async_copy(x_ref.at[pl.ds(first, 2 * HALO), :], low_scr, sem)
    copy.start()
    reads = (lax.broadcasted_iota(jnp.int32, (slots, n_req), 0) == read_ref[...]).astype(BF16)
    for row in range(STATE // 2):
        held = lax.dot_general(
            reads, store_ref[row * LANES : (row + 1) * LANES, :].astype(BF16), (((0,), (1,)), ((), ())),
            preferred_element_type=F32,
        )
        tiles_scr[pl.ds(row, n_req, stride=CHUNK), :] = held
    for row in range(edge_rows):
        edge = edge_ref[row * HALF : (row + 1) * HALF, :]
        held = lax.dot_general(
            reads, jnp.concatenate([edge, edge], axis=0), (((0,), (1,)), ((), ())), preferred_element_type=F32
        )
        tiles_scr[pl.ds(EDGE_AT + row, n_req, stride=CHUNK), :] = held
    for row in range(NEXT_AT + edge_rows, CHUNK):
        tiles_scr[pl.ds(row, n_req, stride=CHUNK), :] = jnp.zeros((n_req, LANES), F32)
    copy.wait()
    rows_scr[...] = low_scr[...].astype(F32)
    for row in range(edge_rows):
        line = rows_scr[pl.ds(last - first + row, 1), :]
        for req in range(n_req):
            at = req // 2 * LANES
            tiles_scr[req * CHUNK + NEXT_AT + row : req * CHUNK + NEXT_AT + row + 1, :] = line[:, at : at + LANES]
    out_ref[...] = tiles_scr[...].astype(BF16).reshape(out_ref.shape)


def pack(length, read_slot, store, edges, x):
    n_req = read_slot.shape[0]
    channels = x.shape[1]
    whole = lambda *_: (0, 0)
    return pl.pallas_call(
        pack_kernel,
        grid_spec=pltpu.PrefetchScalarGridSpec(
            num_scalar_prefetch=1,
            grid=(1,),
            in_specs=[
                pl.BlockSpec((1, n_req), whole),
                pl.BlockSpec(store.shape, whole),
                pl.BlockSpec(edges.shape, whole),
                pl.BlockSpec(memory_space=pl.ANY),
            ],
            out_specs=pl.BlockSpec((n_req, CHUNK, LANES), lambda *_: (0, 0, 0)),
            scratch_shapes=[
                pltpu.VMEM((n_req * CHUNK, LANES), F32),
                pltpu.VMEM((2 * HALO, channels), BF16),
                pltpu.VMEM((2 * HALO, channels), F32),
                pltpu.SemaphoreType.DMA,
            ],
        ),
        out_shape=jax.ShapeDtypeStruct((n_req, CHUNK, LANES), BF16),
        compiler_params=pltpu.CompilerParams(vmem_limit_bytes=VMEM_LIMIT),
        name="pack",
    )(length, read_slot.reshape(1, n_req), store, edges, x)


def conv_block(prev, x_ref, weight_ref, bias_ref, select_hbm, mixed_ref, part_ref, send_ref, rows_scr, select_ref, sems):
    rows = x_ref.shape[0]
    groups = x_ref.shape[1] // LANES
    is_first = pl.program_id(0) == 0
    height = select_ref.shape[0] // FETCHES
    copies = [
        pltpu.make_async_copy(
            select_hbm.at[k * height : (k + 1) * height, :], select_ref.at[k * height : (k + 1) * height, :], sems.at[k]
        )
        for k in range(FETCHES)
    ]

    @pl.when(is_first)
    def _():
        for copy in copies:
            copy.start()

    def some_groups(step, _):
        for k in range(GROUPS_AT_ONCE):
            group = step * GROUPS_AT_ONCE + k
            at = pl.ds(pl.multiple_of(group * LANES, LANES), LANES)
            scr = rows_scr.at[k]
            scr[0:HALO, :] = prev(group)
            scr[HALO : HALO + rows, :] = x_ref[:, at].astype(F32)
            total = bias_ref[:, at] + weight_ref[CONV - 1 : CONV, at] * scr[HALO : HALO + rows, :]
            for tap in range(CONV - 1):
                first = HALO - (CONV - 1) + tap
                total = total + weight_ref[tap : tap + 1, at] * scr[first : first + rows, :]
            mixed_ref[:, at] = silu(total).astype(BF16)
        return 0

    lax.fori_loop(0, groups // GROUPS_AT_ONCE, some_groups, 0)

    @pl.when(is_first)
    def _():
        for copy in copies:
            copy.wait()

    part = lax.dot_general(
        select_ref[...], mixed_ref[...], (((1,), (1,)), ((), ())), preferred_element_type=F32
    ).T
    part_ref[...] = part
    send_ref[...] = part.astype(BF16)


def late_kernel(prev_ref, x_ref, weight_ref, bias_ref, select_ref, mixed_ref, part_ref, send_ref, *scr):
    prev = lambda group: prev_ref[:, pl.ds(pl.multiple_of(group * LANES, LANES), LANES)].astype(F32)
    conv_block(prev, x_ref, weight_ref, bias_ref, select_ref, mixed_ref, part_ref, send_ref, *scr)


def early_kernel(
    hit_ref, arrived_ref, x_ref, weight_ref, bias_ref, select_ref, late_ref, mixed_ref, part_ref, send_ref, start_ref,
    tiles_scr, edge_scr, *scr
):
    del late_ref
    hit = hit_ref[0] > 0
    n_req = arrived_ref.shape[0]
    pairs = n_req // 2
    tiles = arrived_ref[...].astype(F32).reshape(n_req * CHUNK, LANES)
    tiles_scr[...] = jnp.where(hit, tiles, 0.0)
    low = low_half()
    even = lambda row: tiles_scr[pl.ds(row, pairs, stride=2 * CHUNK), :]
    odd = lambda row: tiles_scr[pl.ds(CHUNK + row, pairs, stride=2 * CHUNK), :]
    for row in range(STATE // 2):
        a, b = even(row), odd(row)
        first, second = jnp.where(low, a, pltpu.roll(b, HALF, 1)), jnp.where(low, pltpu.roll(a, HALF, 1), b)
        for block in range(pairs // SUBLANES):
            at = slice(block * SUBLANES, (block + 1) * SUBLANES)
            start_ref[block, 2 * row] = first[at]
            start_ref[block, 2 * row + 1] = second[at]
    edge_scr[...] = jnp.zeros(edge_scr.shape, F32)
    for row in range(CONV - 1):
        edge_scr[pl.ds(HALO - (CONV - 1) + row, pairs, stride=HALO), :] = jnp.where(low, even(EDGE_AT + row), odd(EDGE_AT + row))
    prev = lambda group: edge_scr[pl.ds(pl.multiple_of(group * HALO, HALO), HALO), :]
    conv_block(prev, x_ref, weight_ref, bias_ref, select_ref, mixed_ref, part_ref, send_ref, *scr)


def conv_rows(x, weight, bias, select_t, block, arrived=None, hit=None, late=None):
    rows, channels = x.shape
    wide = select_t.shape[0]
    first = 1 if late is None else 0
    steps = rows // block - 1 if late is None else 1
    fixed = lambda *_: (0, 0)
    at = lambda i, *_: (first + i, 0)
    in_specs = [
        pl.BlockSpec((block, channels), at),
        pl.BlockSpec((CONV, channels), fixed),
        pl.BlockSpec((1, channels), fixed),
        pl.BlockSpec(memory_space=pl.ANY),
    ]
    out_specs = [pl.BlockSpec((block, channels), at)] + [pl.BlockSpec((block, wide), lambda i, *_: (i, 0))] * 2
    out_shape = [
        jax.ShapeDtypeStruct((rows, channels), BF16),
        jax.ShapeDtypeStruct((steps * block, wide), F32),
        jax.ShapeDtypeStruct((steps * block, wide), BF16),
    ]
    scratch = [
        pltpu.VMEM((GROUPS_AT_ONCE, HALO + block, LANES), F32),
        pltpu.VMEM(select_t.shape, BF16),
        pltpu.SemaphoreType.DMA((FETCHES,)),
    ]
    operands = [x, weight, bias, select_t]
    aliases = {}
    if late is None:
        kernel, name, scalars = late_kernel, "conv_late", []
        in_specs = [
            pl.BlockSpec((HALO, channels), lambda i, *_: ((first + i) * (block // HALO) - 1, 0))
        ] + in_specs
        operands = [x] + operands
    else:
        kernel, name, scalars = early_kernel, "conv_early", [hit]
        n_req = arrived.shape[0]
        in_specs = [pl.BlockSpec(arrived.shape, lambda *_: (0, 0, 0))] + in_specs + [pl.BlockSpec(memory_space=pl.ANY)]
        operands = [arrived] + operands + [late]
        aliases = {6: 0}
        start_shape = (channels // WIDE, STATE, SUBLANES, LANES)
        out_specs.append(pl.BlockSpec(start_shape, lambda *_: (0, 0, 0, 0)))
        out_shape.append(jax.ShapeDtypeStruct(start_shape, F32))
        scratch = [
            pltpu.VMEM((n_req * CHUNK, LANES), F32),
            pltpu.VMEM((channels // LANES * HALO, LANES), F32),
        ] + scratch
    return pl.pallas_call(
        kernel,
        grid_spec=pltpu.PrefetchScalarGridSpec(
            num_scalar_prefetch=len(scalars),
            grid=(steps,),
            in_specs=in_specs,
            out_specs=out_specs,
            scratch_shapes=scratch,
        ),
        out_shape=out_shape,
        input_output_aliases=aliases,
        compiler_params=pltpu.CompilerParams(vmem_limit_bytes=VMEM_LIMIT),
        cost_estimate=pl.CostEstimate(
            flops=2 * steps * block * channels * wide,
            bytes_accessed=steps * block * channels * 24,
            transcendentals=2 * steps * block * channels,
        ),
        name=name,
    )(*scalars, *operands)


def scan_kernel(length_ref, *refs):
    early_refs, late_refs, refs = refs[:EARLY_PARTS], refs[EARLY_PARTS : EARLY_PARTS + 2], refs[EARLY_PARTS + 2 :]
    step_ref, bias_ref, decay_ref, skip_ref, mixed_ref, gate_ref, start_ref, *refs = refs
    out_ref, end_ref, norm_scr, wide_scr, value_scr, state_scr, rate_scr, back_scr, *lines = refs
    sizes, drives, scans = lines[0:2], lines[2:4], lines[4:6]
    rows = mixed_ref.shape[0]
    pairs = rows // HALO

    @pl.when(pl.program_id(0) == 0)
    def _():
        shape = (4 * STATE, 2 * STATE * LANES)
        source = lax.broadcasted_iota(jnp.int32, shape, 0) % (2 * STATE)
        spread = (source == lax.broadcasted_iota(jnp.int32, shape, 1) // LANES).astype(BF16)
        done = 0
        for sum_ref, *more_refs in (early_refs, late_refs):
            for first in range(0, sum_ref.shape[0], LANES):
                here = slice(first, first + LANES)
                there = slice(done, done + LANES)
                done += LANES
                projected = sum_ref[here, :]
                for more_ref in more_refs:
                    projected = projected + more_ref[here, :].astype(F32)
                low = projected[:, :RANK]
                scale = lax.rsqrt(jnp.mean(low * low, axis=-1, keepdims=True) + 1e-06)
                norm_scr[there, :] = (low * scale).astype(BF16)
                picks = projected[:, RANK:]
                high = picks.astype(BF16)
                both = jnp.concatenate([high, (picks - high.astype(F32)).astype(BF16)], axis=1)
                wide_scr[there, :] = jnp.dot(both, spread, preferred_element_type=F32)

    state_scr[...] = start_ref[0]
    rate = -jnp.exp(decay_ref[...]) * LOG2E
    for sub in range(SUBLANES):
        rate_scr[pl.ds(sub, STATE, stride=SUBLANES), :] = rate[:, sub * LANES : (sub + 1) * LANES]
    for first in range(0, rows, LANES):
        here = slice(first, first + LANES)
        value_scr[here, :] = jnp.dot(norm_scr[here, :], step_ref[...], preferred_element_type=F32)
    rates = [rate_scr[n * SUBLANES : (n + 1) * SUBLANES, :] for n in range(STATE)]
    row_in_tile = lax.broadcasted_iota(jnp.int32, (SUBLANES, LANES), 0)
    left = length_ref[0]

    def steps_of(pair, tile):
        first = pl.multiple_of(pair * HALO, HALO)
        live = row_in_tile < left - first - tile * SUBLANES
        for sub in range(SUBLANES):
            at = slice(sub * LANES, (sub + 1) * LANES)
            value = value_scr[pl.ds(first + tile * SUBLANES, SUBLANES), at] + bias_ref[:, at]
            small = jnp.exp2(jnp.abs(value) * -LOG2E)
            soft = jnp.where(small < 4e-3, small - 0.5 * small * small, jnp.log(1.0 + small))
            size = jnp.where(live, jnp.maximum(value, 0.0) + soft, 0.0)
            mixed = mixed_ref[pl.ds(first, HALO), at].astype(F32)[tile * SUBLANES : (tile + 1) * SUBLANES]
            sizes[tile][pl.ds(sub, SUBLANES, stride=SUBLANES), :] = size
            drives[tile][pl.ds(sub, SUBLANES, stride=SUBLANES), :] = size * mixed

    def advance(state, pair, tile):
        state = list(state)
        first = pl.multiple_of(pair * HALO + tile * SUBLANES, SUBLANES)
        picks = wide_scr.at[pl.ds(first, SUBLANES), :]
        for position in range(SUBLANES):
            here = slice(position * SUBLANES, (position + 1) * SUBLANES)
            size_row, drive_row = sizes[tile][here, :], drives[tile][here, :]
            sums = [None, None]
            for n in range(STATE):
                b = jnp.broadcast_to(picks[position : position + 1, n * LANES : (n + 1) * LANES], (SUBLANES, LANES))
                m = STATE + n
                c = jnp.broadcast_to(picks[position : position + 1, m * LANES : (m + 1) * LANES], (SUBLANES, LANES))
                state[n] = jnp.exp2(size_row * rates[n]) * state[n] + b * drive_row
                term = c * state[n]
                sums[n % 2] = term if sums[n % 2] is None else sums[n % 2] + term
            scans[tile][here, :] = sums[0] + sums[1]
        return tuple(state)

    def gate_of(pair):
        first = pl.multiple_of(pair * HALO, HALO)
        here = pl.ds(first, HALO)
        for sub in range(SUBLANES):
            at = slice(sub * LANES, (sub + 1) * LANES)
            scanned = jnp.concatenate(
                [scans[tile][pl.ds(sub, SUBLANES, stride=SUBLANES), :] for tile in range(2)], axis=0
            )
            value = scanned + skip_ref[:, at] * mixed_ref[here, at].astype(F32)
            value = value * silu(gate_ref[here, at].astype(F32))
            live = jnp.concatenate([row_in_tile, row_in_tile + SUBLANES], axis=0) < left - first
            out_ref[here, at] = jnp.where(live, value, 0.0).astype(BF16)

    def one_pair(pair, state):
        gate_of(jnp.maximum(pair - 1, 0))
        steps_of(pair, 1)
        state = advance(state, pair, 0)
        steps_of(jnp.minimum(pair + 1, pairs - 1), 0)
        return advance(state, pair, 1)

    def some_pairs(step, state):
        for k in range(PAIRS):
            state = one_pair(step * PAIRS + k, state)
        return state

    steps_of(0, 0)
    state = lax.fori_loop(0, pairs // PAIRS, some_pairs, tuple(state_scr[n] for n in range(STATE)))
    gate_of(pairs - 1)

    low = low_half()
    for row in range(STATE // 2):
        a, b = state[2 * row], state[2 * row + 1]
        even = jnp.where(low, a, pltpu.roll(b, HALF, 1))
        odd = jnp.where(low, pltpu.roll(a, HALF, 1), b)
        back_scr[pl.ds(row, SUBLANES, stride=2 * SUBLANES), :] = even
        back_scr[pl.ds(SUBLANES + row, SUBLANES, stride=2 * SUBLANES), :] = odd
    end_ref[...] = back_scr[...].astype(BF16).reshape(end_ref.shape)


def scan_rows(length, parts, step_weight, step_bias, decay_log, skip_gain, mixed, gate, start):
    rows, channels = mixed.shape
    blocks = channels // WIDE
    by_channel = lambda c, *_: (0, c)
    per_block = WIDE // HALF
    return pl.pallas_call(
        scan_kernel,
        grid_spec=pltpu.PrefetchScalarGridSpec(
            num_scalar_prefetch=1,
            grid=(blocks,),
            in_specs=[pl.BlockSpec(part.shape, lambda c, *_: (0, 0)) for part in parts]
            + [
                pl.BlockSpec((RANK, WIDE), by_channel),
                pl.BlockSpec((1, WIDE), by_channel),
                pl.BlockSpec((STATE, WIDE), by_channel),
                pl.BlockSpec((1, WIDE), by_channel),
                pl.BlockSpec((rows, WIDE), by_channel),
                pl.BlockSpec((rows, WIDE), by_channel),
                pl.BlockSpec((1, STATE, SUBLANES, LANES), lambda c, *_: (c, 0, 0, 0)),
            ],
            out_specs=[
                pl.BlockSpec((rows, WIDE), by_channel),
                pl.BlockSpec((per_block, SUBLANES, LANES), lambda c, *_: (c, 0, 0)),
            ],
            scratch_shapes=[
                pltpu.VMEM((rows, RANK), BF16),
                pltpu.VMEM((rows, 2 * STATE * LANES), F32),
                pltpu.VMEM((rows, WIDE), F32),
                pltpu.VMEM((STATE, SUBLANES, LANES), F32),
                pltpu.VMEM((STATE * SUBLANES, LANES), F32),
                pltpu.VMEM((per_block * SUBLANES, LANES), F32),
            ]
            + [pltpu.VMEM((SUBLANES * SUBLANES, LANES), F32)] * 6,
        ),
        out_shape=[
            jax.ShapeDtypeStruct(gate.shape, BF16),
            jax.ShapeDtypeStruct((blocks * per_block, SUBLANES, LANES), BF16),
        ],
        compiler_params=pltpu.CompilerParams(vmem_limit_bytes=VMEM_LIMIT),
        cost_estimate=pl.CostEstimate(
            flops=2 * rows * channels * RANK + 100 * rows * channels * STATE,
            bytes_accessed=rows * channels * 8,
            transcendentals=rows * channels * STATE,
        ),
        name="scan_rows",
    )(length, *parts, step_weight, step_bias, decay_log, skip_gain, mixed, gate, start)


def save_kernel(slot_ref, half_ref, tiles_ref, store_ref, out_ref, tiles_scr, *, n_rows, first_row, halves):
    n_req, chunk, _ = tiles_ref.shape
    slots = store_ref.shape[1]
    saves = slot_ref[...] == lax.broadcasted_iota(jnp.int32, (n_req, slots), 1)
    saved = jnp.max(saves.astype(F32), axis=0, keepdims=True) > 0.0
    saves = saves.astype(BF16)
    tiles = tiles_ref[...].astype(F32).reshape(n_req * chunk, LANES)
    if halves:
        tiles = jnp.where(half_ref[0] > 0, pltpu.roll(tiles, HALF, 1), tiles)
    tiles_scr[...] = tiles
    height = HALF if halves else LANES
    for row in range(n_rows):
        new = tiles_scr[pl.ds(first_row + row, n_req, stride=chunk), :].astype(BF16)
        new = lax.dot_general(new, saves, (((0,), (0,)), ((), ())), preferred_element_type=F32)[:height]
        at = slice(row * height, (row + 1) * height)
        out_ref[at, :] = jnp.where(saved, new, store_ref[at, :].astype(F32)).astype(out_ref.dtype)


def save(save_slot, half, tiles, store, n_rows, first_row, halves):
    n_req, chunk, _ = tiles.shape
    whole = lambda *_: (0, 0)
    return pl.pallas_call(
        functools.partial(save_kernel, n_rows=n_rows, first_row=first_row, halves=halves),
        grid=(1,),
        in_specs=[
            pl.BlockSpec((n_req, 1), whole),
            pl.BlockSpec(memory_space=pltpu.SMEM),
            pl.BlockSpec(tiles.shape, lambda *_: (0, 0, 0)),
            pl.BlockSpec(store.shape, whole),
        ],
        out_specs=pl.BlockSpec(store.shape, whole),
        out_shape=jax.ShapeDtypeStruct(store.shape, store.dtype),
        scratch_shapes=[pltpu.VMEM((n_req * chunk, LANES), F32)],
        compiler_params=pltpu.CompilerParams(vmem_limit_bytes=VMEM_LIMIT if halves else SMALL_LIMIT),
        name="save",
    )(save_slot.reshape(n_req, 1), half, tiles, store)


def local(
    n_tp,
    conv_input,
    gate_input,
    conv_weight,
    conv_bias,
    select_weight,
    step_weight,
    step_bias,
    decay_log,
    skip_gain,
    store_state,
    store_edge,
    read_slot,
    save_slot,
    cache_hit,
    suffix_length,
):
    local_rows, channels = conv_input.shape
    slots, _, _, stripe = store_state.shape
    edge_rows = CONV - 1
    store = store_state.transpose(1, 2, 3, 0).reshape(STATE * stripe, slots)
    edges = store_edge.transpose(1, 2, 3, 0).reshape(edge_rows * stripe, slots)
    outgoing = pack(suffix_length, read_slot, store, edges, conv_input)
    outgoing, conv_bias = lax.optimization_barrier((outgoing, conv_bias.reshape(1, channels)))
    arrived = lax.all_to_all(outgoing, "req", split_axis=0, concat_axis=0, tiled=True)

    select_t = select_weight.T
    step_bias = step_bias.reshape(1, channels)
    skip_gain = skip_gain.reshape(1, channels)
    block = local_rows // 4
    conv = functools.partial(conv_rows, conv_input, conv_weight, conv_bias, select_t, block)
    inner = [(d, d ^ 1) for d in range(n_tp)]
    outer = [(d, n_tp - 1 - d) for d in range(n_tp)]
    late, late_part, late_sent = conv()
    late_got = lax.ppermute(late_sent, "tp", outer)
    mixed, early_part, early_sent, start = conv(arrived, cache_hit, late)
    more = [lax.ppermute(early_sent, "tp", [(d, (d + k) % n_tp) for d in range(n_tp)]) for k in range(1, n_tp)]
    late_got, early_sent = lax.optimization_barrier((late_got, early_sent))
    late_total = late_part + late_got.astype(F32)
    late_parts = [late_total, lax.ppermute(late_total.astype(BF16), "tp", inner)]
    half = (lax.axis_index("req") % 2).astype(jnp.int32).reshape(1)
    new_edges = save(save_slot, half, arrived, edges, edge_rows, NEXT_AT, True)
    new_edges, *parts = lax.optimization_barrier((new_edges, early_part, *more, *late_parts))
    out, back = scan_rows(
        suffix_length, parts, step_weight, step_bias, decay_log, skip_gain, mixed, gate_input, start
    )
    back = lax.all_to_all(back, "req", split_axis=0, concat_axis=0, tiled=True)
    new_store = save(save_slot, half, back, store, STATE // 2, 0, False)
    new_state = new_store.reshape(1, STATE, stripe, slots).transpose(3, 0, 1, 2)
    new_edge_store = new_edges.reshape(1, edge_rows, stripe, slots).transpose(3, 0, 1, 2)
    return (out, new_state, new_edge_store)


def solution(mesh):
    placed = (
        P("req", "tp"),
        P("req", "tp"),
        P(None, "tp"),
        P("tp"),
        P("tp", None),
        P(None, "tp"),
        P("tp"),
        P(None, "tp"),
        P("tp"),
        P(None, "req", None, "tp"),
        P(None, "req", None, "tp"),
        P(),
        P(),
        P("req"),
        P("req"),
    )
    return jax.shard_map(
        functools.partial(local, mesh.shape["tp"]),
        mesh=mesh,
        in_specs=placed,
        out_specs=(P("req", "tp"), P(None, "req", None, "tp"), P(None, "req", None, "tp")),
        check_vma=False,
    )
```

```python
import functools

import jax
import jax.numpy as jnp
from jax import lax
from jax.experimental import pallas as pl
from jax.experimental.pallas import tpu as pltpu
from jax.sharding import PartitionSpec as P

STATE = 16
CONV = 4
RANK = 256
HALO = 16
WIDE = 1024
LANES = 128
SUBLANES = 8
LOG2E = 1.4426950408889634
F32 = jnp.float32
BF16 = jnp.bfloat16
HALF = 64
EDGE_AT = 8
NEXT_AT = 11
CHUNK = 16
FETCHES = 6
GROUPS_AT_ONCE = 4
PAIRS = 2
VMEM_LIMIT = 60 * 1024 * 1024
SMALL_LIMIT = 24 * 1024 * 1024


def low_half():
    return lax.broadcasted_iota(jnp.int32, (1, LANES), 1) < HALF


def silu(v):
    half = 0.5 * v
    return half + half * jnp.tanh(half)


def pack_kernel(length_ref, read_ref, store_ref, edge_ref, x_ref, out_ref, tiles_scr, low_scr, rows_scr, sem):
    n_req = read_ref.shape[1]
    slots = store_ref.shape[1]
    edge_rows = CONV - 1
    last = length_ref[0] - edge_rows
    first = pl.multiple_of(jnp.minimum(last // HALO * HALO, x_ref.shape[0] - 2 * HALO), HALO)
    copy = pltpu.make_async_copy(x_ref.at[pl.ds(first, 2 * HALO), :], low_scr, sem)
    copy.start()
    reads = (lax.broadcasted_iota(jnp.int32, (slots, n_req), 0) == read_ref[...]).astype(BF16)
    for row in range(STATE // 2):
        held = lax.dot_general(
            reads, store_ref[row * LANES : (row + 1) * LANES, :].astype(BF16), (((0,), (1,)), ((), ())),
            preferred_element_type=F32,
        )
        tiles_scr[pl.ds(row, n_req, stride=CHUNK), :] = held
    for row in range(edge_rows):
        edge = edge_ref[row * HALF : (row + 1) * HALF, :]
        held = lax.dot_general(
            reads, jnp.concatenate([edge, edge], axis=0), (((0,), (1,)), ((), ())), preferred_element_type=F32
        )
        tiles_scr[pl.ds(EDGE_AT + row, n_req, stride=CHUNK), :] = held
    for row in range(NEXT_AT + edge_rows, CHUNK):
        tiles_scr[pl.ds(row, n_req, stride=CHUNK), :] = jnp.zeros((n_req, LANES), F32)
    copy.wait()
    rows_scr[...] = low_scr[...].astype(F32)
    for row in range(edge_rows):
        line = rows_scr[pl.ds(last - first + row, 1), :]
        for req in range(n_req):
            at = req // 2 * LANES
            tiles_scr[req * CHUNK + NEXT_AT + row : req * CHUNK + NEXT_AT + row + 1, :] = line[:, at : at + LANES]
    out_ref[...] = tiles_scr[...].astype(BF16).reshape(out_ref.shape)


def pack(length, read_slot, store, edges, x):
    n_req = read_slot.shape[0]
    channels = x.shape[1]
    whole = lambda *_: (0, 0)
    return pl.pallas_call(
        pack_kernel,
        grid_spec=pltpu.PrefetchScalarGridSpec(
            num_scalar_prefetch=1,
            grid=(1,),
            in_specs=[
                pl.BlockSpec((1, n_req), whole),
                pl.BlockSpec(store.shape, whole),
                pl.BlockSpec(edges.shape, whole),
                pl.BlockSpec(memory_space=pl.ANY),
            ],
            out_specs=pl.BlockSpec((n_req, CHUNK, LANES), lambda *_: (0, 0, 0)),
            scratch_shapes=[
                pltpu.VMEM((n_req * CHUNK, LANES), F32),
                pltpu.VMEM((2 * HALO, channels), BF16),
                pltpu.VMEM((2 * HALO, channels), F32),
                pltpu.SemaphoreType.DMA,
            ],
        ),
        out_shape=jax.ShapeDtypeStruct((n_req, CHUNK, LANES), BF16),
        compiler_params=pltpu.CompilerParams(vmem_limit_bytes=VMEM_LIMIT),
        name="pack",
    )(length, read_slot.reshape(1, n_req), store, edges, x)


def conv_block(prev, x_ref, weight_ref, bias_ref, select_hbm, mixed_ref, part_ref, send_ref, rows_scr, select_ref, sems):
    rows = x_ref.shape[0]
    groups = x_ref.shape[1] // LANES
    is_first = pl.program_id(0) == 0
    height = select_ref.shape[0] // FETCHES
    copies = [
        pltpu.make_async_copy(
            select_hbm.at[k * height : (k + 1) * height, :], select_ref.at[k * height : (k + 1) * height, :], sems.at[k]
        )
        for k in range(FETCHES)
    ]

    @pl.when(is_first)
    def _():
        for copy in copies:
            copy.start()

    def some_groups(step, _):
        for k in range(GROUPS_AT_ONCE):
            group = step * GROUPS_AT_ONCE + k
            at = pl.ds(pl.multiple_of(group * LANES, LANES), LANES)
            scr = rows_scr.at[k]
            scr[0:HALO, :] = prev(group)
            scr[HALO : HALO + rows, :] = x_ref[:, at].astype(F32)
            total = bias_ref[:, at] + weight_ref[CONV - 1 : CONV, at] * scr[HALO : HALO + rows, :]
            for tap in range(CONV - 1):
                first = HALO - (CONV - 1) + tap
                total = total + weight_ref[tap : tap + 1, at] * scr[first : first + rows, :]
            mixed_ref[:, at] = silu(total).astype(BF16)
        return 0

    lax.fori_loop(0, groups // GROUPS_AT_ONCE, some_groups, 0)

    @pl.when(is_first)
    def _():
        for copy in copies:
            copy.wait()

    part = lax.dot_general(
        select_ref[...], mixed_ref[...], (((1,), (1,)), ((), ())), preferred_element_type=F32
    ).T
    part_ref[...] = part
    send_ref[...] = part.astype(BF16)


def late_kernel(prev_ref, x_ref, weight_ref, bias_ref, select_ref, mixed_ref, part_ref, send_ref, *scr):
    prev = lambda group: prev_ref[:, pl.ds(pl.multiple_of(group * LANES, LANES), LANES)].astype(F32)
    conv_block(prev, x_ref, weight_ref, bias_ref, select_ref, mixed_ref, part_ref, send_ref, *scr)


def early_kernel(
    hit_ref, arrived_ref, x_ref, weight_ref, bias_ref, select_ref, late_ref, mixed_ref, part_ref, send_ref, start_ref,
    tiles_scr, edge_scr, *scr
):
    del late_ref
    hit = hit_ref[0] > 0
    n_req = arrived_ref.shape[0]
    pairs = n_req // 2
    tiles = arrived_ref[...].astype(F32).reshape(n_req * CHUNK, LANES)
    tiles_scr[...] = jnp.where(hit, tiles, 0.0)
    low = low_half()
    even = lambda row: tiles_scr[pl.ds(row, pairs, stride=2 * CHUNK), :]
    odd = lambda row: tiles_scr[pl.ds(CHUNK + row, pairs, stride=2 * CHUNK), :]
    for row in range(STATE // 2):
        a, b = even(row), odd(row)
        first, second = jnp.where(low, a, pltpu.roll(b, HALF, 1)), jnp.where(low, pltpu.roll(a, HALF, 1), b)
        for block in range(pairs // SUBLANES):
            at = slice(block * SUBLANES, (block + 1) * SUBLANES)
            start_ref[block, 2 * row] = first[at]
            start_ref[block, 2 * row + 1] = second[at]
    edge_scr[...] = jnp.zeros(edge_scr.shape, F32)
    for row in range(CONV - 1):
        edge_scr[pl.ds(HALO - (CONV - 1) + row, pairs, stride=HALO), :] = jnp.where(low, even(EDGE_AT + row), odd(EDGE_AT + row))
    prev = lambda group: edge_scr[pl.ds(pl.multiple_of(group * HALO, HALO), HALO), :]
    conv_block(prev, x_ref, weight_ref, bias_ref, select_ref, mixed_ref, part_ref, send_ref, *scr)


def conv_rows(x, weight, bias, select_t, block, arrived=None, hit=None, late=None):
    rows, channels = x.shape
    wide = select_t.shape[0]
    first = 1 if late is None else 0
    steps = rows // block - 1 if late is None else 1
    fixed = lambda *_: (0, 0)
    at = lambda i, *_: (first + i, 0)
    in_specs = [
        pl.BlockSpec((block, channels), at),
        pl.BlockSpec((CONV, channels), fixed),
        pl.BlockSpec((1, channels), fixed),
        pl.BlockSpec(memory_space=pl.ANY),
    ]
    out_specs = [pl.BlockSpec((block, channels), at)] + [pl.BlockSpec((block, wide), lambda i, *_: (i, 0))] * 2
    out_shape = [
        jax.ShapeDtypeStruct((rows, channels), BF16),
        jax.ShapeDtypeStruct((steps * block, wide), F32),
        jax.ShapeDtypeStruct((steps * block, wide), BF16),
    ]
    scratch = [
        pltpu.VMEM((GROUPS_AT_ONCE, HALO + block, LANES), F32),
        pltpu.VMEM(select_t.shape, BF16),
        pltpu.SemaphoreType.DMA((FETCHES,)),
    ]
    operands = [x, weight, bias, select_t]
    aliases = {}
    if late is None:
        kernel, name, scalars = late_kernel, "conv_late", []
        in_specs = [
            pl.BlockSpec((HALO, channels), lambda i, *_: ((first + i) * (block // HALO) - 1, 0))
        ] + in_specs
        operands = [x] + operands
    else:
        kernel, name, scalars = early_kernel, "conv_early", [hit]
        n_req = arrived.shape[0]
        in_specs = [pl.BlockSpec(arrived.shape, lambda *_: (0, 0, 0))] + in_specs + [pl.BlockSpec(memory_space=pl.ANY)]
        operands = [arrived] + operands + [late]
        aliases = {6: 0}
        start_shape = (channels // WIDE, STATE, SUBLANES, LANES)
        out_specs.append(pl.BlockSpec(start_shape, lambda *_: (0, 0, 0, 0)))
        out_shape.append(jax.ShapeDtypeStruct(start_shape, F32))
        scratch = [
            pltpu.VMEM((n_req * CHUNK, LANES), F32),
            pltpu.VMEM((channels // LANES * HALO, LANES), F32),
        ] + scratch
    return pl.pallas_call(
        kernel,
        grid_spec=pltpu.PrefetchScalarGridSpec(
            num_scalar_prefetch=len(scalars),
            grid=(steps,),
            in_specs=in_specs,
            out_specs=out_specs,
            scratch_shapes=scratch,
        ),
        out_shape=out_shape,
        input_output_aliases=aliases,
        compiler_params=pltpu.CompilerParams(vmem_limit_bytes=VMEM_LIMIT),
        cost_estimate=pl.CostEstimate(
            flops=2 * steps * block * channels * wide,
            bytes_accessed=steps * block * channels * 24,
            transcendentals=2 * steps * block * channels,
        ),
        name=name,
    )(*scalars, *operands)


def scan_kernel(length_ref, *refs):
    part_refs, refs = refs[:4], refs[4:]
    step_ref, bias_ref, decay_ref, skip_ref, mixed_ref, gate_ref, start_ref, *refs = refs
    out_ref, end_ref, norm_scr, wide_scr, value_scr, state_scr, rate_scr, back_scr, *lines = refs
    sizes, drives, scans = lines[0:2], lines[2:4], lines[4:6]
    rows = mixed_ref.shape[0]
    pairs = rows // HALO

    @pl.when(pl.program_id(0) == 0)
    def _():
        shape = (4 * STATE, 2 * STATE * LANES)
        source = lax.broadcasted_iota(jnp.int32, shape, 0) % (2 * STATE)
        spread = (source == lax.broadcasted_iota(jnp.int32, shape, 1) // LANES).astype(BF16)
        done = 0
        for sum_ref, more_ref in (part_refs[:2], part_refs[2:]):
            for first in range(0, sum_ref.shape[0], LANES):
                here = slice(first, first + LANES)
                there = slice(done, done + LANES)
                done += LANES
                projected = sum_ref[here, :] + more_ref[here, :].astype(F32)
                low = projected[:, :RANK]
                scale = lax.rsqrt(jnp.mean(low * low, axis=-1, keepdims=True) + 1e-06)
                norm_scr[there, :] = (low * scale).astype(BF16)
                picks = projected[:, RANK:]
                high = picks.astype(BF16)
                both = jnp.concatenate([high, (picks - high.astype(F32)).astype(BF16)], axis=1)
                wide_scr[there, :] = jnp.dot(both, spread, preferred_element_type=F32)

    state_scr[...] = start_ref[0]
    rate = -jnp.exp(decay_ref[...]) * LOG2E
    for sub in range(SUBLANES):
        rate_scr[pl.ds(sub, STATE, stride=SUBLANES), :] = rate[:, sub * LANES : (sub + 1) * LANES]
    for first in range(0, rows, LANES):
        here = slice(first, first + LANES)
        value_scr[here, :] = jnp.dot(norm_scr[here, :], step_ref[...], preferred_element_type=F32)
    rates = [rate_scr[n * SUBLANES : (n + 1) * SUBLANES, :] for n in range(STATE)]
    row_in_tile = lax.broadcasted_iota(jnp.int32, (SUBLANES, LANES), 0)
    left = length_ref[0]

    def steps_of(pair, tile):
        first = pl.multiple_of(pair * HALO, HALO)
        live = row_in_tile < left - first - tile * SUBLANES
        for sub in range(SUBLANES):
            at = slice(sub * LANES, (sub + 1) * LANES)
            value = value_scr[pl.ds(first + tile * SUBLANES, SUBLANES), at] + bias_ref[:, at]
            small = jnp.exp2(jnp.abs(value) * -LOG2E)
            soft = jnp.where(small < 4e-3, small - 0.5 * small * small, jnp.log(1.0 + small))
            size = jnp.where(live, jnp.maximum(value, 0.0) + soft, 0.0)
            mixed = mixed_ref[pl.ds(first, HALO), at].astype(F32)[tile * SUBLANES : (tile + 1) * SUBLANES]
            sizes[tile][pl.ds(sub, SUBLANES, stride=SUBLANES), :] = size
            drives[tile][pl.ds(sub, SUBLANES, stride=SUBLANES), :] = size * mixed

    def advance(state, pair, tile):
        state = list(state)
        first = pl.multiple_of(pair * HALO + tile * SUBLANES, SUBLANES)
        picks = wide_scr.at[pl.ds(first, SUBLANES), :]
        for position in range(SUBLANES):
            here = slice(position * SUBLANES, (position + 1) * SUBLANES)
            size_row, drive_row = sizes[tile][here, :], drives[tile][here, :]
            sums = [None, None]
            for n in range(STATE):
                b = jnp.broadcast_to(picks[position : position + 1, n * LANES : (n + 1) * LANES], (SUBLANES, LANES))
                m = STATE + n
                c = jnp.broadcast_to(picks[position : position + 1, m * LANES : (m + 1) * LANES], (SUBLANES, LANES))
                state[n] = jnp.exp2(size_row * rates[n]) * state[n] + b * drive_row
                term = c * state[n]
                sums[n % 2] = term if sums[n % 2] is None else sums[n % 2] + term
            scans[tile][here, :] = sums[0] + sums[1]
        return tuple(state)

    def gate_of(pair):
        first = pl.multiple_of(pair * HALO, HALO)
        here = pl.ds(first, HALO)
        for sub in range(SUBLANES):
            at = slice(sub * LANES, (sub + 1) * LANES)
            scanned = jnp.concatenate(
                [scans[tile][pl.ds(sub, SUBLANES, stride=SUBLANES), :] for tile in range(2)], axis=0
            )
            value = scanned + skip_ref[:, at] * mixed_ref[here, at].astype(F32)
            value = value * silu(gate_ref[here, at].astype(F32))
            live = jnp.concatenate([row_in_tile, row_in_tile + SUBLANES], axis=0) < left - first
            out_ref[here, at] = jnp.where(live, value, 0.0).astype(BF16)

    def one_pair(pair, state):
        gate_of(jnp.maximum(pair - 1, 0))
        steps_of(pair, 1)
        state = advance(state, pair, 0)
        steps_of(jnp.minimum(pair + 1, pairs - 1), 0)
        return advance(state, pair, 1)

    def some_pairs(step, state):
        for k in range(PAIRS):
            state = one_pair(step * PAIRS + k, state)
        return state

    steps_of(0, 0)
    state = lax.fori_loop(0, pairs // PAIRS, some_pairs, tuple(state_scr[n] for n in range(STATE)))
    gate_of(pairs - 1)

    low = low_half()
    for row in range(STATE // 2):
        a, b = state[2 * row], state[2 * row + 1]
        even = jnp.where(low, a, pltpu.roll(b, HALF, 1))
        odd = jnp.where(low, pltpu.roll(a, HALF, 1), b)
        back_scr[pl.ds(row, SUBLANES, stride=2 * SUBLANES), :] = even
        back_scr[pl.ds(SUBLANES + row, SUBLANES, stride=2 * SUBLANES), :] = odd
    end_ref[...] = back_scr[...].astype(BF16).reshape(end_ref.shape)


def scan_rows(length, parts, step_weight, step_bias, decay_log, skip_gain, mixed, gate, start):
    rows, channels = mixed.shape
    blocks = channels // WIDE
    by_channel = lambda c, *_: (0, c)
    per_block = WIDE // HALF
    return pl.pallas_call(
        scan_kernel,
        grid_spec=pltpu.PrefetchScalarGridSpec(
            num_scalar_prefetch=1,
            grid=(blocks,),
            in_specs=[pl.BlockSpec(part.shape, lambda c, *_: (0, 0)) for part in parts]
            + [
                pl.BlockSpec((RANK, WIDE), by_channel),
                pl.BlockSpec((1, WIDE), by_channel),
                pl.BlockSpec((STATE, WIDE), by_channel),
                pl.BlockSpec((1, WIDE), by_channel),
                pl.BlockSpec((rows, WIDE), by_channel),
                pl.BlockSpec((rows, WIDE), by_channel),
                pl.BlockSpec((1, STATE, SUBLANES, LANES), lambda c, *_: (c, 0, 0, 0)),
            ],
            out_specs=[
                pl.BlockSpec((rows, WIDE), by_channel),
                pl.BlockSpec((per_block, SUBLANES, LANES), lambda c, *_: (c, 0, 0)),
            ],
            scratch_shapes=[
                pltpu.VMEM((rows, RANK), BF16),
                pltpu.VMEM((rows, 2 * STATE * LANES), F32),
                pltpu.VMEM((rows, WIDE), F32),
                pltpu.VMEM((STATE, SUBLANES, LANES), F32),
                pltpu.VMEM((STATE * SUBLANES, LANES), F32),
                pltpu.VMEM((per_block * SUBLANES, LANES), F32),
            ]
            + [pltpu.VMEM((SUBLANES * SUBLANES, LANES), F32)] * 6,
        ),
        out_shape=[
            jax.ShapeDtypeStruct(gate.shape, BF16),
            jax.ShapeDtypeStruct((blocks * per_block, SUBLANES, LANES), BF16),
        ],
        compiler_params=pltpu.CompilerParams(vmem_limit_bytes=VMEM_LIMIT),
        cost_estimate=pl.CostEstimate(
            flops=2 * rows * channels * RANK + 100 * rows * channels * STATE,
            bytes_accessed=rows * channels * 8,
            transcendentals=rows * channels * STATE,
        ),
        name="scan_rows",
    )(length, *parts, step_weight, step_bias, decay_log, skip_gain, mixed, gate, start)


def save_kernel(slot_ref, half_ref, tiles_ref, store_ref, out_ref, tiles_scr, *, n_rows, first_row, halves):
    n_req, chunk, _ = tiles_ref.shape
    slots = store_ref.shape[1]
    saves = slot_ref[...] == lax.broadcasted_iota(jnp.int32, (n_req, slots), 1)
    saved = jnp.max(saves.astype(F32), axis=0, keepdims=True) > 0.0
    saves = saves.astype(BF16)
    tiles = tiles_ref[...].astype(F32).reshape(n_req * chunk, LANES)
    if halves:
        tiles = jnp.where(half_ref[0] > 0, pltpu.roll(tiles, HALF, 1), tiles)
    tiles_scr[...] = tiles
    height = HALF if halves else LANES
    for row in range(n_rows):
        new = tiles_scr[pl.ds(first_row + row, n_req, stride=chunk), :].astype(BF16)
        new = lax.dot_general(new, saves, (((0,), (0,)), ((), ())), preferred_element_type=F32)[:height]
        at = slice(row * height, (row + 1) * height)
        out_ref[at, :] = jnp.where(saved, new, store_ref[at, :].astype(F32)).astype(out_ref.dtype)


def save(save_slot, half, tiles, store, n_rows, first_row, halves):
    n_req, chunk, _ = tiles.shape
    whole = lambda *_: (0, 0)
    return pl.pallas_call(
        functools.partial(save_kernel, n_rows=n_rows, first_row=first_row, halves=halves),
        grid=(1,),
        in_specs=[
            pl.BlockSpec((n_req, 1), whole),
            pl.BlockSpec(memory_space=pltpu.SMEM),
            pl.BlockSpec(tiles.shape, lambda *_: (0, 0, 0)),
            pl.BlockSpec(store.shape, whole),
        ],
        out_specs=pl.BlockSpec(store.shape, whole),
        out_shape=jax.ShapeDtypeStruct(store.shape, store.dtype),
        scratch_shapes=[pltpu.VMEM((n_req * chunk, LANES), F32)],
        compiler_params=pltpu.CompilerParams(vmem_limit_bytes=SMALL_LIMIT),
        name="save",
    )(save_slot.reshape(n_req, 1), half, tiles, store)


def pairwise(part, sent, orders):
    total = part + lax.ppermute(sent, "tp", orders[0]).astype(F32)
    return [total, lax.ppermute(total.astype(BF16), "tp", orders[1])]


def local(
    n_tp,
    conv_input,
    gate_input,
    conv_weight,
    conv_bias,
    select_weight,
    step_weight,
    step_bias,
    decay_log,
    skip_gain,
    store_state,
    store_edge,
    read_slot,
    save_slot,
    cache_hit,
    suffix_length,
):
    local_rows, channels = conv_input.shape
    slots, _, _, stripe = store_state.shape
    edge_rows = CONV - 1
    store = store_state.transpose(1, 2, 3, 0).reshape(STATE * stripe, slots)
    edges = store_edge.transpose(1, 2, 3, 0).reshape(edge_rows * stripe, slots)
    outgoing = pack(suffix_length, read_slot, store, edges, conv_input)
    arrived = lax.all_to_all(outgoing, "req", split_axis=0, concat_axis=0, tiled=True)

    select_t = select_weight.T
    conv_bias = conv_bias.reshape(1, channels)
    step_bias = step_bias.reshape(1, channels)
    skip_gain = skip_gain.reshape(1, channels)
    block = local_rows // 4
    conv = functools.partial(conv_rows, conv_input, conv_weight, conv_bias, select_t, block)
    inner = [(d, d ^ 1) for d in range(n_tp)]
    outer = [(d, n_tp - 1 - d) for d in range(n_tp)]
    late, late_part, late_sent = conv()
    late_parts = pairwise(late_part, late_sent, (outer, inner))
    mixed, early_part, early_sent, start = conv(arrived, cache_hit, late)
    half = (lax.axis_index("req") % 2).astype(jnp.int32).reshape(1)
    new_edges = save(save_slot, half, arrived, edges, edge_rows, NEXT_AT, True)
    early_got = lax.ppermute(early_sent, "tp", inner)
    new_edges, early_got = lax.optimization_barrier((new_edges, early_got))
    early_total = early_part + early_got.astype(F32)
    parts = [early_total, lax.ppermute(early_total.astype(BF16), "tp", outer)] + late_parts
    out, back = scan_rows(
        suffix_length, parts, step_weight, step_bias, decay_log, skip_gain, mixed, gate_input, start
    )
    back = lax.all_to_all(back, "req", split_axis=0, concat_axis=0, tiled=True)
    new_store = save(save_slot, half, back, store, STATE // 2, 0, False)
    new_state = new_store.reshape(1, STATE, stripe, slots).transpose(3, 0, 1, 2)
    new_edge_store = new_edges.reshape(1, edge_rows, stripe, slots).transpose(3, 0, 1, 2)
    return (out, new_state, new_edge_store)


def solution(mesh):
    placed = (
        P("req", "tp"),
        P("req", "tp"),
        P(None, "tp"),
        P("tp"),
        P("tp", None),
        P(None, "tp"),
        P("tp"),
        P(None, "tp"),
        P("tp"),
        P(None, "req", None, "tp"),
        P(None, "req", None, "tp"),
        P(),
        P(),
        P("req"),
        P("req"),
    )
    return jax.shard_map(
        functools.partial(local, mesh.shape["tp"]),
        mesh=mesh,
        in_specs=placed,
        out_specs=(P("req", "tp"), P(None, "req", None, "tp"), P(None, "req", None, "tp")),
        check_vma=False,
    )
```

```python
import functools

import jax
import jax.numpy as jnp
from jax import lax
from jax.experimental import pallas as pl
from jax.experimental.pallas import tpu as pltpu
from jax.sharding import PartitionSpec as P

STATE = 16
CONV = 4
RANK = 256
HALO = 16
WIDE = 1024
LANES = 128
SUBLANES = 8
LOG2E = 1.4426950408889634
F32 = jnp.float32
BF16 = jnp.bfloat16
HALF = 64
EDGE_AT = 8
NEXT_AT = 11
CHUNK = 16
FETCHES = 6
GROUPS_AT_ONCE = 8
PAIRS = 2
VMEM_LIMIT = 60 * 1024 * 1024
SMALL_LIMIT = 24 * 1024 * 1024


def low_half():
    return lax.broadcasted_iota(jnp.int32, (1, LANES), 1) < HALF


def silu(v):
    half = 0.5 * v
    return half + half * jnp.tanh(half)


def pack_kernel(length_ref, read_ref, store_ref, edge_ref, x_ref, out_ref, tiles_scr, low_scr, rows_scr, sem):
    n_req = read_ref.shape[1]
    slots = store_ref.shape[1]
    edge_rows = CONV - 1
    last = length_ref[0] - edge_rows
    first = pl.multiple_of(jnp.minimum(last // HALO * HALO, x_ref.shape[0] - 2 * HALO), HALO)
    copy = pltpu.make_async_copy(x_ref.at[pl.ds(first, 2 * HALO), :], low_scr, sem)
    copy.start()
    reads = (lax.broadcasted_iota(jnp.int32, (slots, n_req), 0) == read_ref[...]).astype(BF16)
    for row in range(STATE // 2):
        held = lax.dot_general(
            reads, store_ref[row * LANES : (row + 1) * LANES, :].astype(BF16), (((0,), (1,)), ((), ())),
            preferred_element_type=F32,
        )
        tiles_scr[pl.ds(row, n_req, stride=CHUNK), :] = held
    for row in range(edge_rows):
        edge = edge_ref[row * HALF : (row + 1) * HALF, :]
        held = lax.dot_general(
            reads, jnp.concatenate([edge, edge], axis=0), (((0,), (1,)), ((), ())), preferred_element_type=F32
        )
        tiles_scr[pl.ds(EDGE_AT + row, n_req, stride=CHUNK), :] = held
    for row in range(NEXT_AT + edge_rows, CHUNK):
        tiles_scr[pl.ds(row, n_req, stride=CHUNK), :] = jnp.zeros((n_req, LANES), F32)
    copy.wait()
    rows_scr[...] = low_scr[...].astype(F32)
    for row in range(edge_rows):
        line = rows_scr[pl.ds(last - first + row, 1), :]
        for req in range(n_req):
            at = req // 2 * LANES
            tiles_scr[req * CHUNK + NEXT_AT + row : req * CHUNK + NEXT_AT + row + 1, :] = line[:, at : at + LANES]
    out_ref[...] = tiles_scr[...].astype(BF16).reshape(out_ref.shape)


def pack(length, read_slot, store, edges, x):
    n_req = read_slot.shape[0]
    channels = x.shape[1]
    whole = lambda *_: (0, 0)
    return pl.pallas_call(
        pack_kernel,
        grid_spec=pltpu.PrefetchScalarGridSpec(
            num_scalar_prefetch=1,
            grid=(1,),
            in_specs=[
                pl.BlockSpec((1, n_req), whole),
                pl.BlockSpec(store.shape, whole),
                pl.BlockSpec(edges.shape, whole),
                pl.BlockSpec(memory_space=pl.ANY),
            ],
            out_specs=pl.BlockSpec((n_req, CHUNK, LANES), lambda *_: (0, 0, 0)),
            scratch_shapes=[
                pltpu.VMEM((n_req * CHUNK, LANES), F32),
                pltpu.VMEM((2 * HALO, channels), BF16),
                pltpu.VMEM((2 * HALO, channels), F32),
                pltpu.SemaphoreType.DMA,
            ],
        ),
        out_shape=jax.ShapeDtypeStruct((n_req, CHUNK, LANES), BF16),
        compiler_params=pltpu.CompilerParams(vmem_limit_bytes=VMEM_LIMIT),
        name="pack",
    )(length, read_slot.reshape(1, n_req), store, edges, x)


def conv_block(prev, x_ref, weight_ref, bias_ref, select_hbm, mixed_ref, part_ref, send_ref, rows_scr, select_ref, sems):
    rows = x_ref.shape[0]
    groups = x_ref.shape[1] // LANES
    is_first = pl.program_id(0) == 0
    height = select_ref.shape[0] // FETCHES
    copies = [
        pltpu.make_async_copy(
            select_hbm.at[k * height : (k + 1) * height, :], select_ref.at[k * height : (k + 1) * height, :], sems.at[k]
        )
        for k in range(FETCHES)
    ]

    @pl.when(is_first)
    def _():
        for copy in copies:
            copy.start()

    def some_groups(step, _):
        for k in range(GROUPS_AT_ONCE):
            group = step * GROUPS_AT_ONCE + k
            at = pl.ds(pl.multiple_of(group * LANES, LANES), LANES)
            scr = rows_scr.at[k]
            scr[0:HALO, :] = prev(group)
            scr[HALO : HALO + rows, :] = x_ref[:, at].astype(F32)
            total = bias_ref[:, at] + weight_ref[CONV - 1 : CONV, at] * scr[HALO : HALO + rows, :]
            for tap in range(CONV - 1):
                first = HALO - (CONV - 1) + tap
                total = total + weight_ref[tap : tap + 1, at] * scr[first : first + rows, :]
            mixed_ref[:, at] = silu(total).astype(BF16)
        return 0

    lax.fori_loop(0, groups // GROUPS_AT_ONCE, some_groups, 0)

    @pl.when(is_first)
    def _():
        for copy in copies:
            copy.wait()

    part = lax.dot_general(
        select_ref[...], mixed_ref[...], (((1,), (1,)), ((), ())), preferred_element_type=F32
    ).T
    part_ref[...] = part
    send_ref[...] = part.astype(BF16)


def late_kernel(prev_ref, x_ref, weight_ref, bias_ref, select_ref, mixed_ref, part_ref, send_ref, *scr):
    prev = lambda group: prev_ref[:, pl.ds(pl.multiple_of(group * LANES, LANES), LANES)].astype(F32)
    conv_block(prev, x_ref, weight_ref, bias_ref, select_ref, mixed_ref, part_ref, send_ref, *scr)


def early_kernel(
    hit_ref, arrived_ref, x_ref, weight_ref, bias_ref, select_ref, late_ref, mixed_ref, part_ref, send_ref, start_ref,
    tiles_scr, edge_scr, *scr
):
    del late_ref
    hit = hit_ref[0] > 0
    n_req = arrived_ref.shape[0]
    pairs = n_req // 2
    tiles = arrived_ref[...].astype(F32).reshape(n_req * CHUNK, LANES)
    tiles_scr[...] = jnp.where(hit, tiles, 0.0)
    low = low_half()
    even = lambda row: tiles_scr[pl.ds(row, pairs, stride=2 * CHUNK), :]
    odd = lambda row: tiles_scr[pl.ds(CHUNK + row, pairs, stride=2 * CHUNK), :]
    for row in range(STATE // 2):
        a, b = even(row), odd(row)
        first, second = jnp.where(low, a, pltpu.roll(b, HALF, 1)), jnp.where(low, pltpu.roll(a, HALF, 1), b)
        for block in range(pairs // SUBLANES):
            at = slice(block * SUBLANES, (block + 1) * SUBLANES)
            start_ref[block, 2 * row] = first[at]
            start_ref[block, 2 * row + 1] = second[at]
    edge_scr[...] = jnp.zeros(edge_scr.shape, F32)
    for row in range(CONV - 1):
        edge_scr[pl.ds(HALO - (CONV - 1) + row, pairs, stride=HALO), :] = jnp.where(low, even(EDGE_AT + row), odd(EDGE_AT + row))
    prev = lambda group: edge_scr[pl.ds(pl.multiple_of(group * HALO, HALO), HALO), :]
    conv_block(prev, x_ref, weight_ref, bias_ref, select_ref, mixed_ref, part_ref, send_ref, *scr)


def conv_rows(x, weight, bias, select_t, block, arrived=None, hit=None, late=None):
    rows, channels = x.shape
    wide = select_t.shape[0]
    first = 1 if late is None else 0
    steps = rows // block - 1 if late is None else 1
    fixed = lambda *_: (0, 0)
    at = lambda i, *_: (first + i, 0)
    in_specs = [
        pl.BlockSpec((block, channels), at),
        pl.BlockSpec((CONV, channels), fixed),
        pl.BlockSpec((1, channels), fixed),
        pl.BlockSpec(memory_space=pl.ANY),
    ]
    out_specs = [pl.BlockSpec((block, channels), at)] + [pl.BlockSpec((block, wide), lambda i, *_: (i, 0))] * 2
    out_shape = [
        jax.ShapeDtypeStruct((rows, channels), BF16),
        jax.ShapeDtypeStruct((steps * block, wide), F32),
        jax.ShapeDtypeStruct((steps * block, wide), BF16),
    ]
    scratch = [
        pltpu.VMEM((GROUPS_AT_ONCE, HALO + block, LANES), F32),
        pltpu.VMEM(select_t.shape, BF16),
        pltpu.SemaphoreType.DMA((FETCHES,)),
    ]
    operands = [x, weight, bias, select_t]
    aliases = {}
    if late is None:
        kernel, name, scalars = late_kernel, "conv_late", []
        in_specs = [
            pl.BlockSpec((HALO, channels), lambda i, *_: ((first + i) * (block // HALO) - 1, 0))
        ] + in_specs
        operands = [x] + operands
    else:
        kernel, name, scalars = early_kernel, "conv_early", [hit]
        n_req = arrived.shape[0]
        in_specs = [pl.BlockSpec(arrived.shape, lambda *_: (0, 0, 0))] + in_specs + [pl.BlockSpec(memory_space=pl.ANY)]
        operands = [arrived] + operands + [late]
        aliases = {6: 0}
        start_shape = (channels // WIDE, STATE, SUBLANES, LANES)
        out_specs.append(pl.BlockSpec(start_shape, lambda *_: (0, 0, 0, 0)))
        out_shape.append(jax.ShapeDtypeStruct(start_shape, F32))
        scratch = [
            pltpu.VMEM((n_req * CHUNK, LANES), F32),
            pltpu.VMEM((channels // LANES * HALO, LANES), F32),
        ] + scratch
    return pl.pallas_call(
        kernel,
        grid_spec=pltpu.PrefetchScalarGridSpec(
            num_scalar_prefetch=len(scalars),
            grid=(steps,),
            in_specs=in_specs,
            out_specs=out_specs,
            scratch_shapes=scratch,
        ),
        out_shape=out_shape,
        input_output_aliases=aliases,
        compiler_params=pltpu.CompilerParams(vmem_limit_bytes=VMEM_LIMIT),
        cost_estimate=pl.CostEstimate(
            flops=2 * steps * block * channels * wide,
            bytes_accessed=steps * block * channels * 24,
            transcendentals=2 * steps * block * channels,
        ),
        name=name,
    )(*scalars, *operands)


def scan_kernel(length_ref, *refs):
    part_refs, refs = refs[:4], refs[4:]
    step_ref, bias_ref, decay_ref, skip_ref, mixed_ref, gate_ref, start_ref, *refs = refs
    out_ref, end_ref, norm_scr, wide_scr, value_scr, state_scr, rate_scr, back_scr, *lines = refs
    sizes, drives, scans = lines[0:2], lines[2:4], lines[4:6]
    rows = mixed_ref.shape[0]
    pairs = rows // HALO

    @pl.when(pl.program_id(0) == 0)
    def _():
        shape = (4 * STATE, 2 * STATE * LANES)
        source = lax.broadcasted_iota(jnp.int32, shape, 0) % (2 * STATE)
        spread = (source == lax.broadcasted_iota(jnp.int32, shape, 1) // LANES).astype(BF16)
        done = 0
        for sum_ref, more_ref in (part_refs[:2], part_refs[2:]):
            for first in range(0, sum_ref.shape[0], LANES):
                here = slice(first, first + LANES)
                there = slice(done, done + LANES)
                done += LANES
                projected = sum_ref[here, :] + more_ref[here, :].astype(F32)
                low = projected[:, :RANK]
                scale = lax.rsqrt(jnp.mean(low * low, axis=-1, keepdims=True) + 1e-06)
                norm_scr[there, :] = (low * scale).astype(BF16)
                picks = projected[:, RANK:]
                high = picks.astype(BF16)
                both = jnp.concatenate([high, (picks - high.astype(F32)).astype(BF16)], axis=1)
                wide_scr[there, :] = jnp.dot(both, spread, preferred_element_type=F32)

    state_scr[...] = start_ref[0]
    rate = -jnp.exp(decay_ref[...]) * LOG2E
    for sub in range(SUBLANES):
        rate_scr[pl.ds(sub, STATE, stride=SUBLANES), :] = rate[:, sub * LANES : (sub + 1) * LANES]
    for first in range(0, rows, LANES):
        here = slice(first, first + LANES)
        value_scr[here, :] = jnp.dot(norm_scr[here, :], step_ref[...], preferred_element_type=F32)
    rates = [rate_scr[n * SUBLANES : (n + 1) * SUBLANES, :] for n in range(STATE)]
    row_in_tile = lax.broadcasted_iota(jnp.int32, (SUBLANES, LANES), 0)
    left = length_ref[0]

    def steps_of(pair, tile):
        first = pl.multiple_of(pair * HALO, HALO)
        live = row_in_tile < left - first - tile * SUBLANES
        for sub in range(SUBLANES):
            at = slice(sub * LANES, (sub + 1) * LANES)
            value = value_scr[pl.ds(first + tile * SUBLANES, SUBLANES), at] + bias_ref[:, at]
            small = jnp.exp2(jnp.abs(value) * -LOG2E)
            soft = jnp.where(small < 4e-3, small - 0.5 * small * small, jnp.log(1.0 + small))
            size = jnp.where(live, jnp.maximum(value, 0.0) + soft, 0.0)
            mixed = mixed_ref[pl.ds(first, HALO), at].astype(F32)[tile * SUBLANES : (tile + 1) * SUBLANES]
            sizes[tile][pl.ds(sub, SUBLANES, stride=SUBLANES), :] = size
            drives[tile][pl.ds(sub, SUBLANES, stride=SUBLANES), :] = size * mixed

    def advance(state, pair, tile):
        state = list(state)
        first = pl.multiple_of(pair * HALO + tile * SUBLANES, SUBLANES)
        picks = wide_scr.at[pl.ds(first, SUBLANES), :]
        for position in range(SUBLANES):
            here = slice(position * SUBLANES, (position + 1) * SUBLANES)
            size_row, drive_row = sizes[tile][here, :], drives[tile][here, :]
            sums = [None, None]
            for n in range(STATE):
                b = jnp.broadcast_to(picks[position : position + 1, n * LANES : (n + 1) * LANES], (SUBLANES, LANES))
                m = STATE + n
                c = jnp.broadcast_to(picks[position : position + 1, m * LANES : (m + 1) * LANES], (SUBLANES, LANES))
                state[n] = jnp.exp2(size_row * rates[n]) * state[n] + b * drive_row
                term = c * state[n]
                sums[n % 2] = term if sums[n % 2] is None else sums[n % 2] + term
            scans[tile][here, :] = sums[0] + sums[1]
        return tuple(state)

    def gate_of(pair):
        first = pl.multiple_of(pair * HALO, HALO)
        here = pl.ds(first, HALO)
        for sub in range(SUBLANES):
            at = slice(sub * LANES, (sub + 1) * LANES)
            scanned = jnp.concatenate(
                [scans[tile][pl.ds(sub, SUBLANES, stride=SUBLANES), :] for tile in range(2)], axis=0
            )
            value = scanned + skip_ref[:, at] * mixed_ref[here, at].astype(F32)
            value = value * silu(gate_ref[here, at].astype(F32))
            live = jnp.concatenate([row_in_tile, row_in_tile + SUBLANES], axis=0) < left - first
            out_ref[here, at] = jnp.where(live, value, 0.0).astype(BF16)

    def one_pair(pair, state):
        gate_of(jnp.maximum(pair - 1, 0))
        steps_of(pair, 1)
        state = advance(state, pair, 0)
        steps_of(jnp.minimum(pair + 1, pairs - 1), 0)
        return advance(state, pair, 1)

    def some_pairs(step, state):
        for k in range(PAIRS):
            state = one_pair(step * PAIRS + k, state)
        return state

    steps_of(0, 0)
    state = lax.fori_loop(0, pairs // PAIRS, some_pairs, tuple(state_scr[n] for n in range(STATE)))
    gate_of(pairs - 1)

    low = low_half()
    for row in range(STATE // 2):
        a, b = state[2 * row], state[2 * row + 1]
        even = jnp.where(low, a, pltpu.roll(b, HALF, 1))
        odd = jnp.where(low, pltpu.roll(a, HALF, 1), b)
        back_scr[pl.ds(row, SUBLANES, stride=2 * SUBLANES), :] = even
        back_scr[pl.ds(SUBLANES + row, SUBLANES, stride=2 * SUBLANES), :] = odd
    end_ref[...] = back_scr[...].astype(BF16).reshape(end_ref.shape)


def scan_rows(length, parts, step_weight, step_bias, decay_log, skip_gain, mixed, gate, start):
    rows, channels = mixed.shape
    blocks = channels // WIDE
    by_channel = lambda c, *_: (0, c)
    per_block = WIDE // HALF
    return pl.pallas_call(
        scan_kernel,
        grid_spec=pltpu.PrefetchScalarGridSpec(
            num_scalar_prefetch=1,
            grid=(blocks,),
            in_specs=[pl.BlockSpec(part.shape, lambda c, *_: (0, 0)) for part in parts]
            + [
                pl.BlockSpec((RANK, WIDE), by_channel),
                pl.BlockSpec((1, WIDE), by_channel),
                pl.BlockSpec((STATE, WIDE), by_channel),
                pl.BlockSpec((1, WIDE), by_channel),
                pl.BlockSpec((rows, WIDE), by_channel),
                pl.BlockSpec((rows, WIDE), by_channel),
                pl.BlockSpec((1, STATE, SUBLANES, LANES), lambda c, *_: (c, 0, 0, 0)),
            ],
            out_specs=[
                pl.BlockSpec((rows, WIDE), by_channel),
                pl.BlockSpec((per_block, SUBLANES, LANES), lambda c, *_: (c, 0, 0)),
            ],
            scratch_shapes=[
                pltpu.VMEM((rows, RANK), BF16),
                pltpu.VMEM((rows, 2 * STATE * LANES), F32),
                pltpu.VMEM((rows, WIDE), F32),
                pltpu.VMEM((STATE, SUBLANES, LANES), F32),
                pltpu.VMEM((STATE * SUBLANES, LANES), F32),
                pltpu.VMEM((per_block * SUBLANES, LANES), F32),
            ]
            + [pltpu.VMEM((SUBLANES * SUBLANES, LANES), F32)] * 6,
        ),
        out_shape=[
            jax.ShapeDtypeStruct(gate.shape, BF16),
            jax.ShapeDtypeStruct((blocks * per_block, SUBLANES, LANES), BF16),
        ],
        compiler_params=pltpu.CompilerParams(vmem_limit_bytes=VMEM_LIMIT),
        cost_estimate=pl.CostEstimate(
            flops=2 * rows * channels * RANK + 100 * rows * channels * STATE,
            bytes_accessed=rows * channels * 8,
            transcendentals=rows * channels * STATE,
        ),
        name="scan_rows",
    )(length, *parts, step_weight, step_bias, decay_log, skip_gain, mixed, gate, start)


def save_kernel(slot_ref, half_ref, tiles_ref, store_ref, out_ref, tiles_scr, *, n_rows, first_row, halves):
    n_req, chunk, _ = tiles_ref.shape
    slots = store_ref.shape[1]
    saves = slot_ref[...] == lax.broadcasted_iota(jnp.int32, (n_req, slots), 1)
    saved = jnp.max(saves.astype(F32), axis=0, keepdims=True) > 0.0
    saves = saves.astype(BF16)
    tiles = tiles_ref[...].astype(F32).reshape(n_req * chunk, LANES)
    if halves:
        tiles = jnp.where(half_ref[0] > 0, pltpu.roll(tiles, HALF, 1), tiles)
    tiles_scr[...] = tiles
    height = HALF if halves else LANES
    for row in range(n_rows):
        new = tiles_scr[pl.ds(first_row + row, n_req, stride=chunk), :].astype(BF16)
        new = lax.dot_general(new, saves, (((0,), (0,)), ((), ())), preferred_element_type=F32)[:height]
        at = slice(row * height, (row + 1) * height)
        out_ref[at, :] = jnp.where(saved, new, store_ref[at, :].astype(F32)).astype(out_ref.dtype)


def save(save_slot, half, tiles, store, n_rows, first_row, halves):
    n_req, chunk, _ = tiles.shape
    whole = lambda *_: (0, 0)
    return pl.pallas_call(
        functools.partial(save_kernel, n_rows=n_rows, first_row=first_row, halves=halves),
        grid=(1,),
        in_specs=[
            pl.BlockSpec((n_req, 1), whole),
            pl.BlockSpec(memory_space=pltpu.SMEM),
            pl.BlockSpec(tiles.shape, lambda *_: (0, 0, 0)),
            pl.BlockSpec(store.shape, whole),
        ],
        out_specs=pl.BlockSpec(store.shape, whole),
        out_shape=jax.ShapeDtypeStruct(store.shape, store.dtype),
        scratch_shapes=[pltpu.VMEM((n_req * chunk, LANES), F32)],
        compiler_params=pltpu.CompilerParams(vmem_limit_bytes=SMALL_LIMIT),
        name="save",
    )(save_slot.reshape(n_req, 1), half, tiles, store)


def pairwise(part, sent, orders):
    total = part + lax.ppermute(sent, "tp", orders[0]).astype(F32)
    return [total, lax.ppermute(total.astype(BF16), "tp", orders[1])]


def local(
    n_tp,
    conv_input,
    gate_input,
    conv_weight,
    conv_bias,
    select_weight,
    step_weight,
    step_bias,
    decay_log,
    skip_gain,
    store_state,
    store_edge,
    read_slot,
    save_slot,
    cache_hit,
    suffix_length,
):
    local_rows, channels = conv_input.shape
    slots, _, _, stripe = store_state.shape
    edge_rows = CONV - 1
    store = store_state.transpose(1, 2, 3, 0).reshape(STATE * stripe, slots)
    edges = store_edge.transpose(1, 2, 3, 0).reshape(edge_rows * stripe, slots)
    outgoing = pack(suffix_length, read_slot, store, edges, conv_input)
    arrived = lax.all_to_all(outgoing, "req", split_axis=0, concat_axis=0, tiled=True)

    select_t = select_weight.T
    conv_bias = conv_bias.reshape(1, channels)
    step_bias = step_bias.reshape(1, channels)
    skip_gain = skip_gain.reshape(1, channels)
    block = local_rows // 4
    conv = functools.partial(conv_rows, conv_input, conv_weight, conv_bias, select_t, block)
    inner = [(d, d ^ 1) for d in range(n_tp)]
    outer = [(d, n_tp - 1 - d) for d in range(n_tp)]
    late, late_part, late_sent = conv()
    late_parts = pairwise(late_part, late_sent, (outer, inner))
    mixed, early_part, early_sent, start = conv(arrived, cache_hit, late)
    parts = pairwise(early_part, early_sent, (inner, outer)) + late_parts
    half = (lax.axis_index("req") % 2).astype(jnp.int32).reshape(1)
    new_edges = save(save_slot, half, arrived, edges, edge_rows, NEXT_AT, True)
    new_edges, *parts = lax.optimization_barrier((new_edges, *parts))
    out, back = scan_rows(
        suffix_length, parts, step_weight, step_bias, decay_log, skip_gain, mixed, gate_input, start
    )
    back = lax.all_to_all(back, "req", split_axis=0, concat_axis=0, tiled=True)
    new_store = save(save_slot, half, back, store, STATE // 2, 0, False)
    new_state = new_store.reshape(1, STATE, stripe, slots).transpose(3, 0, 1, 2)
    new_edge_store = new_edges.reshape(1, edge_rows, stripe, slots).transpose(3, 0, 1, 2)
    return (out, new_state, new_edge_store)


def solution(mesh):
    placed = (
        P("req", "tp"),
        P("req", "tp"),
        P(None, "tp"),
        P("tp"),
        P("tp", None),
        P(None, "tp"),
        P("tp"),
        P(None, "tp"),
        P("tp"),
        P(None, "req", None, "tp"),
        P(None, "req", None, "tp"),
        P(),
        P(),
        P("req"),
        P("req"),
    )
    return jax.shard_map(
        functools.partial(local, mesh.shape["tp"]),
        mesh=mesh,
        in_specs=placed,
        out_specs=(P("req", "tp"), P(None, "req", None, "tp"), P(None, "req", None, "tp")),
        check_vma=False,
    )
```
